32 devices in a mesh: cells: 8 (over z, y), samp: 4 (over x, core).
Axes of the slice: x: 2, y: 2, z: 4, core: 2. Of those that a mesh axis runs over, the one named last changes fastest.
Arguments:
- snapshots: bfloat16 [16384, 4096], P('cells', 'samp'), may hold values from -6 to 6
- left_slow: bfloat16 [120, 256], P(None, 'cells'), may hold values from -0.375 to 0.375
- left_fast: bfloat16 [120, 64], replicated, may hold values from -0.75 to 0.75
- right_slow: bfloat16 [150, 128], P(None, 'samp'), may hold values from -0.5 to 0.5
- right_fast: bfloat16 [150, 32], replicated, may hold values from -1 to 1
Outputs:
- range_sketch: float32 [16384, 150], P(('cells', 'samp'))
- core: float32 [150, 4096], P(None, ('samp', 'cells'))
The draws below stay inside these ranges and needn't reach their ends.
All inputs are finite; a program needn't handle non-finite values.
Results may differ from the reference program's by a relative error of at most 0.012.
The reference program's roundings to bfloat16 on the way (of `psi` and `omega`) count: a program that leaves them out, or rounds other values in their place, can miss the bound.
Values sent between devices are 32-bit elements; how exact they have to be, the bound alone decides.
No kernel may reach another device: no remote copies, remote signals or barrier semaphores. Data moves between devices by JAX's collectives and lax.ppermute only.
A program may use at most 64 MiB of HBM per device.

```python
import jax
import jax.numpy as jnp
from jax import lax

R_L = 120
R_R = 150
CB = 64
SB = 32
CA = 256
SA = 128
CELLS = 16384
SAMPLES = 4096


def raised(array, rng, source, target, blocks, factor):
    owner, partner = [(jnp.arange(array.shape[dim]) // (array.shape[dim] // blocks)).reshape([-1 if axis == dim else 1 for axis in range(array.ndim)]) for dim in (source, target)]
    chosen = jax.random.permutation(rng, blocks)[partner]
    strong = (owner == chosen) | (owner == (partner + blocks // 2) % blocks)
    return jnp.where(strong, factor * array, array)


def shard_levels(own_key, extent, pieces, least, largest):
    def one(axis_at, blocks):
        steps = jax.random.uniform(jax.random.fold_in(jax.random.fold_in(own_key, 6), axis_at), (blocks,), jnp.float32, least / len(pieces), largest / len(pieces))
        return jnp.repeat(jnp.exp(steps), extent[axis_at] // blocks).reshape((-1,) + (1,) * (len(extent) - axis_at - 1))

    gain = one(*pieces[0])
    for cut in pieces[1:]:
        gain = gain * one(*cut)
    return gain


def noise(rng, shape, scale, limit, shards=(), held_as=jnp.bfloat16):
    gain = shard_levels(rng, shape, shards, -0.22, 0.18) if shards else 1.0
    entries = jax.random.normal(rng, shape, jnp.float32) * scale * gain
    return jnp.minimum(jnp.maximum(entries, -limit), limit).astype(held_as)


def gaussian_with(rng, extent, deviation, reach, shards, heavy, held_as=jnp.bfloat16):
    values = deviation * jax.random.normal(rng, extent, jnp.float32)
    if shards:
        values = values * shard_levels(rng, extent, shards, -0.22, 0.18)
    return jnp.clip(raised(values, jax.random.fold_in(rng, 3), *heavy), -reach, reach).astype(held_as)


def setup_inputs(seed: int = 0) -> dict:
    splits = jax.random.split(jax.random.key(seed), 6)
    snapshots = gaussian_with(splits[0], (CELLS, SAMPLES), 1.0, 6.0, ((0, 8), (1, 4)), (0, 1, 8, 2.0))
    left_slow = noise(splits[1], (R_L, CA), CA ** -0.5, 0.375, ((1, 8),))
    left_fast = noise(splits[2], (R_L, CB), CB ** -0.5, 0.75)
    right_slow = noise(splits[3], (R_R, SA), SA ** -0.5, 0.5, ((1, 4),))
    right_fast = noise(splits[4], (R_R, SB), SB ** -0.5, 1.0)
    return dict(snapshots=snapshots, left_slow=left_slow, left_fast=left_fast, right_slow=right_slow, right_fast=right_fast)


def reference(snapshots, left_slow, left_fast, right_slow, right_fast):
    psi = (left_slow.astype(jnp.float32)[:, :, None] * left_fast.astype(jnp.float32)[:, None, :]).reshape(R_L, CA * CB).astype(jnp.bfloat16)
    omega = (right_slow.astype(jnp.float32)[:, :, None] * right_fast.astype(jnp.float32)[:, None, :]).reshape(R_R, SA * SB).astype(jnp.bfloat16)
    left_sketch = jnp.dot(psi.astype(jnp.float32), snapshots.astype(jnp.float32), preferred_element_type=jnp.float32)
    range_sketch = lax.dot_general(snapshots.astype(jnp.float32), omega.astype(jnp.float32), (((1,), (1,)), ((), ())), preferred_element_type=jnp.float32)
    core_input = jnp.dot(left_sketch, omega.astype(jnp.float32).T, precision=lax.Precision.HIGHEST)
    gram = jnp.dot(core_input, core_input.T, precision=lax.Precision.HIGHEST) + 0.5 * jnp.eye(R_L, dtype=jnp.float32)
    factor = jnp.linalg.cholesky(gram)
    solved = jax.scipy.linalg.cho_solve((factor, True), left_sketch)
    core = jnp.dot(core_input.T, solved, precision=lax.Precision.HIGHEST)
    return (range_sketch, core)
```

```python
import jax
import jax.numpy as jnp
from jax import lax
from jax.sharding import PartitionSpec as P

F32 = jnp.float32
HIGHEST = lax.Precision.HIGHEST


def expand(slow, fast):
    rows = slow.shape[0]
    return (
        (slow.astype(F32)[:, :, None] * fast.astype(F32)[:, None, :])
        .reshape(rows, -1)
        .astype(jnp.bfloat16)
    )


def swap(value, axis, size, bit):
    return lax.ppermute(value, axis, [(i, i ^ bit) for i in range(size)])


def bits(size):
    return [1 << b for b in range(size.bit_length() - 1)]


def halve(blocks, axis, size, order):
    count = size.bit_length() - 1
    tail = blocks.shape[1:]
    held = blocks.reshape((2,) * count + tail)
    me = lax.axis_index(axis)
    left = list(bits(size))[::-1]
    for bit in order:
        dim = left.index(bit)
        left.pop(dim)
        mine = (me // bit) % 2
        kept = lax.dynamic_index_in_dim(held, mine, dim, False)
        sent = lax.dynamic_index_in_dim(held, 1 - mine, dim, False)
        held = kept + swap(sent, axis, size, bit)
    return held


def build(sizes):
    cells, samp = sizes["cells"], sizes["samp"]

    def on_device(snapshots, left_slow, left_fast, right_slow, right_fast):
        psi = expand(left_slow, left_fast)
        omega = expand(right_slow, right_fast)
        rank_left, rank_right = psi.shape[0], omega.shape[0]
        left_term = jnp.dot(psi, snapshots, preferred_element_type=F32)
        core_input = lax.dot_general(
            omega.astype(F32), left_term, (((1,), (1,)), ((), ())), precision=HIGHEST
        )
        for axis, size in (("samp", samp), ("cells", cells)):
            for bit in bits(size):
                core_input = core_input + swap(core_input, axis, size, bit)
        range_term = lax.dot_general(
            omega, snapshots, (((1,), (1,)), ((), ())), preferred_element_type=F32
        )
        range_blocks = range_term.reshape(rank_right, samp, -1).transpose(1, 0, 2)
        range_part = halve(range_blocks, "samp", samp, bits(samp)).T
        left_blocks = left_term.reshape(rank_left, cells, -1).transpose(1, 0, 2)
        left_part = halve(left_blocks, "cells", cells, bits(cells))
        gram = lax.dot_general(
            core_input, core_input, (((0,), (0,)), ((), ())), precision=HIGHEST
        ) + 0.5 * jnp.eye(rank_left, dtype=F32)
        factor = jnp.linalg.cholesky(gram)
        solved = jax.scipy.linalg.cho_solve((factor, True), left_part)
        core = jnp.dot(core_input, solved, precision=HIGHEST)
        return (range_part, core)

    return on_device


def solution(mesh):
    placed = (P("cells", "samp"), P(None, "cells"), P(), P(None, "samp"), P())
    return jax.shard_map(
        build(mesh.shape),
        mesh=mesh,
        in_specs=placed,
        out_specs=(P(("cells", "samp"), None), P(None, ("samp", "cells"))),
        check_vma=False,
    )
```

```python
import functools

import jax
import jax.numpy as jnp
from jax import lax
from jax.experimental import pallas as pl
from jax.experimental.pallas import tpu as pltpu
from jax.sharding import PartitionSpec as P

F32 = jnp.float32
BF16 = jnp.bfloat16
HIGHEST = lax.Precision.HIGHEST
SCALE = 2.0**-10
RIDGE = 0.5
VMEM = pl.BlockSpec(memory_space=pltpu.VMEM)
LIMIT = 48 * 2**20


def dot(a, b, a_dim, b_dim, precision=None):
    return lax.dot_general(
        a, b, (((a_dim,), (b_dim,)), ((), ())), precision=precision, preferred_element_type=F32
    )


def expand(slow_t, fast_t, start, width):
    fast_count = fast_t.shape[0]
    column = lax.broadcasted_iota(jnp.int32, (slow_t.shape[0], width), 1) + start
    first = lax.broadcasted_iota(jnp.int32, (slow_t.shape[0], width), 0) * fast_count
    pick_slow = jnp.where((column >= first) & (column < first + fast_count), 1.0, 0.0)
    column = lax.broadcasted_iota(jnp.int32, (fast_count, width), 1) + start
    row = lax.broadcasted_iota(jnp.int32, (fast_count, width), 0)
    pick_fast = jnp.where(lax.rem(column, fast_count) == row, 1.0, 0.0)
    slow = dot(slow_t, pick_slow.astype(BF16), 0, 0)
    fast = dot(fast_t, pick_fast.astype(BF16), 0, 0)
    return (slow * fast).astype(BF16)


def thirds(value):
    high = value.astype(BF16)
    rest = value - high.astype(F32)
    middle = rest.astype(BF16)
    low = (rest - middle.astype(F32)).astype(BF16)
    return high, middle, low


def left_kernel(slow, fast, right_slow, right_fast, block, left, omega, part, total):
    step = pl.program_id(0)
    width = block.shape[0]

    @pl.when(step == 0)
    def _():
        omega[...] = expand(right_slow[...], right_fast[...], 0, block.shape[1])

    psi = expand(slow[...], fast[...], step * width, width)
    term = dot(psi, block[...], 1, 0)

    @pl.when(step == 0)
    def _():
        total[...] = term

    @pl.when(step > 0)
    def _():
        total[...] += term

    @pl.when(step == pl.num_programs(0) - 1)
    def _():
        value = total[...]
        chunk = left.shape[2]
        for c in range(left.shape[0]):
            left[c] = value[:, c * chunk : (c + 1) * chunk]
        rows = omega[...]
        part[...] = sum(dot(rows, third, 1, 1) for third in thirds(value))


def left_sketch(snapshots, left_slow, left_fast, right_slow, right_fast, steps, chunk):
    height, width = snapshots.shape
    rank_left, rank_right = left_slow.shape[0], right_slow.shape[0]
    chunks = width // chunk
    whole = lambda array: pl.BlockSpec(array.shape, lambda i: (0,) * array.ndim)
    factors = [left_slow.T, left_fast.T, right_slow.T, right_fast.T]
    outs = (
        jax.ShapeDtypeStruct((chunks, rank_left, chunk), F32),
        jax.ShapeDtypeStruct((rank_right, width), BF16),
        jax.ShapeDtypeStruct((rank_right, rank_left), F32),
    )
    return pl.pallas_call(
        left_kernel,
        grid=(steps,),
        in_specs=[whole(f) for f in factors]
        + [pl.BlockSpec((height // steps, width), lambda i: (i, 0))],
        out_specs=tuple(whole(o) for o in outs),
        out_shape=outs,
        scratch_shapes=[pltpu.VMEM((rank_left, width), F32)],
        compiler_params=pltpu.CompilerParams(vmem_limit_bytes=LIMIT),
        cost_estimate=pl.CostEstimate(
            flops=2 * rank_left * height * width,
            bytes_accessed=2 * height * width,
            transcendentals=0,
        ),
        name="left_sketch",
    )(*factors, snapshots)


def range_kernel(which, omega, block, out):
    out[0] = dot(omega[...], block[...], 1, 1)


def range_blocks(which, omega, snapshots, blocks, split):
    height, width = snapshots.shape
    rank = omega.shape[0]
    rows = height // blocks
    piece = rows // split
    count = which.shape[0]
    return pl.pallas_call(
        range_kernel,
        grid_spec=pltpu.PrefetchScalarGridSpec(
            num_scalar_prefetch=1,
            grid=(count, split),
            in_specs=[
                pl.BlockSpec((rank, width), lambda i, j, which: (0, 0)),
                pl.BlockSpec((piece, width), lambda i, j, which: (which[i] * split + j, 0)),
            ],
            out_specs=pl.BlockSpec((1, rank, piece), lambda i, j, which: (i, 0, j)),
        ),
        out_shape=jax.ShapeDtypeStruct((count, rank, rows), F32),
        compiler_params=pltpu.CompilerParams(vmem_limit_bytes=LIMIT),
        cost_estimate=pl.CostEstimate(
            flops=2 * rank * count * rows * width,
            bytes_accessed=2 * count * rows * width,
            transcendentals=0,
        ),
        name="range_sketch",
    )(which, omega, snapshots)


def row_of(tile, at):
    return jnp.broadcast_to(tile[at : at + 1, :], tile.shape)


def eliminate(gram):
    size = gram.shape[0]
    lane = lax.broadcasted_iota(jnp.int32, (8, size), 1)
    sub = lax.broadcasted_iota(jnp.int32, (8, size), 0)
    tiles = [gram[i : i + 8] for i in range(0, size, 8)]
    scaled = []
    for t in range(len(tiles)):
        k = 8 * t
        live = range(t, len(tiles))
        column = [
            {i: jnp.broadcast_to(tiles[i][:, k + j : k + j + 1], (8, size)) for i in live}
            for j in range(8)
        ]
        inside = (lane >= k) & (lane < k + 8)
        for i in live:
            tiles[i] = jnp.where(inside, 0.0, tiles[i])
        row = [row_of(tiles[t], j) for j in range(8)]
        weight = [None] * 8
        for p in range(0, 8, 2):
            q = p + 1
            a = row_of(column[p][t], p)
            b = row_of(column[q][t], p)
            c = row_of(column[q][t], q)
            det = a * c - b * b
            inverse = pl.reciprocal(det, approx=True)
            inverse = inverse * (2.0 - det * inverse)
            a, b, c = c * inverse, -b * inverse, a * inverse
            row[p] = jnp.where(lane == k + p, 1.0, row[p])
            row[q] = jnp.where(lane == k + q, 1.0, row[q])
            weight[p] = a * row[p] + b * row[q]
            weight[q] = b * row[p] + c * row[q]
            for j in range(q + 1, 8):
                f, g = row_of(column[j][t], p), row_of(column[j][t], q)
                u, v = a * f + b * g, b * f + c * g
                column[j] = {
                    i: column[j][i] - (column[p][i] * u + column[q][i] * v) for i in live
                }
                row[j] = row[j] - (
                    row_of(column[p][t], j) * weight[p] + row_of(column[q][t], j) * weight[q]
                )
            for i in live[1:]:
                tiles[i] = tiles[i] - (column[p][i] * weight[p] + column[q][i] * weight[q])
        held, out = row[0], weight[0]
        for j in range(1, 8):
            held = jnp.where(sub == j, row[j], held)
            out = jnp.where(sub == j, weight[j], out)
        tiles[t] = held
        scaled.append(out)
    return jnp.concatenate(tiles, 0), jnp.concatenate(scaled, 0)


def factor_kernel(kept, received, side, weight):
    value = (kept[...] + received[...]) * SCALE
    size = value.shape[1]
    i = lax.broadcasted_iota(jnp.int32, (size, size), 0)
    j = lax.broadcasted_iota(jnp.int32, (size, size), 1)
    gram = dot(value, value, 0, 0, HIGHEST) + jnp.where(i == j, RIDGE * SCALE * SCALE, 0.0)
    lower, scaled = eliminate(gram)
    keep = (j >> 1) <= (i >> 1)
    side[...] = dot(value, jnp.where(keep, lower, 0.0), 1, 1, HIGHEST)
    weight[...] = jnp.where(keep, scaled, 0.0) * SCALE


def factor(kept, received):
    size = kept.shape[1]
    return pl.pallas_call(
        factor_kernel,
        out_shape=(
            jax.ShapeDtypeStruct(kept.shape, F32),
            jax.ShapeDtypeStruct((size, size), F32),
        ),
        in_specs=[VMEM, VMEM],
        out_specs=(VMEM, VMEM),
        compiler_params=pltpu.CompilerParams(vmem_limit_bytes=LIMIT),
        cost_estimate=pl.CostEstimate(
            flops=10**10, bytes_accessed=10**5, transcendentals=0
        ),
        name="factor",
    )(kept, received)


def core_kernel(side, weight, kept, received, core):
    left = kept[...] + received[...]
    core[...] = dot(side[...], dot(weight[...], left, 1, 0, HIGHEST), 1, 0, HIGHEST)


def finish(side, weight, kept, received):
    return pl.pallas_call(
        core_kernel,
        out_shape=jax.ShapeDtypeStruct((side.shape[0], kept.shape[1]), F32),
        in_specs=[VMEM] * 4,
        out_specs=VMEM,
        compiler_params=pltpu.CompilerParams(vmem_limit_bytes=LIMIT),
        name="core",
    )(side, weight, kept, received)


def swap(value, axis, size, bit):
    return lax.ppermute(value, axis, [(i, i ^ bit) for i in range(size)])


def bits(size):
    return [1 << b for b in range(size.bit_length() - 1)]


def halve(blocks, axis, size, order):
    count = size.bit_length() - 1
    held = blocks.reshape((2,) * count + blocks.shape[1:])
    me = lax.axis_index(axis)
    dims = bits(size)[::-1]
    kept = received = None
    for bit in order:
        if kept is not None:
            held = kept + received
        dim = dims.index(bit)
        dims.pop(dim)
        mine = (me // bit) % 2
        kept = lax.dynamic_index_in_dim(held, mine, dim, False)
        sent = lax.dynamic_index_in_dim(held, 1 - mine, dim, False)
        received = swap(sent, axis, size, bit)
    return kept, received


def build(sizes):
    cells, samp = sizes["cells"], sizes["samp"]

    def on_device(snapshots, left_slow, left_fast, right_slow, right_fast):
        height, width = snapshots.shape
        share = width // cells
        chunk = share if share % 128 == 0 else width
        chunks, omega, part = left_sketch(
            snapshots, left_slow, left_fast, right_slow, right_fast, 4, chunk
        )
        if chunk != share:
            chunks = chunks[0].reshape(-1, cells, share).transpose(1, 0, 2)

        hops = [("samp", samp, bit) for bit in bits(samp)]
        hops += [("cells", cells, bit) for bit in bits(cells)]
        received = swap(part, *hops[0])
        for hop in hops[1:]:
            part = part + received
            received = swap(part, *hop)

        me = lax.axis_index("samp")
        far = jnp.stack([me ^ 3, me ^ 2])
        near = jnp.stack([me ^ 1, me])
        sent, kept = range_blocks(far, omega, snapshots, samp, 2)
        crossing = swap(kept + swap(sent, "samp", samp, 1), "samp", samp, 2)
        sent, kept = range_blocks(near, omega, snapshots, samp, 2)
        range_part = (kept + swap(sent, "samp", samp, 1) + crossing).T

        left_kept, left_received = halve(chunks, "cells", cells, bits(cells))
        side, weight = factor(part, received)
        core = finish(side, weight, left_kept, left_received)
        return (range_part, core)

    return on_device


def solution(mesh):
    placed = (P("cells", "samp"), P(None, "cells"), P(), P(None, "samp"), P())
    return jax.shard_map(
        build(mesh.shape),
        mesh=mesh,
        in_specs=placed,
        out_specs=(P(("cells", "samp"), None), P(None, ("samp", "cells"))),
        check_vma=False,
    )
```

```python
import functools
import math

import jax
import jax.numpy as jnp
from jax import lax
from jax.experimental import pallas as pl
from jax.experimental.pallas import tpu as pltpu
from jax.sharding import PartitionSpec as P

F32 = jnp.float32
BF16 = jnp.bfloat16
HIGHEST = lax.Precision.HIGHEST
SCALE = 2.0**-10
RIDGE = 0.5
VMEM = pl.BlockSpec(memory_space=pltpu.VMEM)
HBM = pl.BlockSpec(memory_space=pltpu.HBM)
LIMIT = 16 * 2**20
LARGE = 50 * 2**20
AHEAD = 3


def dot(a, b, a_dim, b_dim, precision=None):
    return lax.dot_general(
        a, b, (((a_dim,), (b_dim,)), ((), ())), precision=precision, preferred_element_type=F32
    )


def repeated(factor_t, width, inner, outer):
    count = factor_t.shape[0]
    row = lax.broadcasted_iota(jnp.int32, (count, width), 0)
    column = lax.broadcasted_iota(jnp.int32, (count, width), 1)
    if outer:
        pick = (column >= row * inner) & (column < (row + 1) * inner)
    elif count & (count - 1) == 0:
        pick = (column & (count - 1)) == row
    else:
        pick = lax.rem(column, count) == row
    return dot(factor_t, jnp.where(pick, 1.0, 0.0).astype(BF16), 0, 0)


def expand(slow_t, fast_t):
    inner = fast_t.shape[0]
    width = slow_t.shape[0] * inner
    period = inner * 128 // math.gcd(inner, 128)
    if width % period:
        period = width
    fast = repeated(fast_t, period, 1, False)
    fast = jnp.concatenate([fast] * (width // period), 1)
    return (repeated(slow_t, width, inner, True) * fast).astype(BF16)


def thirds(value):
    high = value.astype(BF16)
    rest = value - high.astype(F32)
    middle = rest.astype(BF16)
    low = (rest - middle.astype(F32)).astype(BF16)
    return high, middle, low


def sketch_kernel(shapes, me, factors, slab, left, part, spans, held, sems):
    count, rows, width = held.shape
    copies = [
        pltpu.make_async_copy(slab.at[pl.ds(i * rows, rows)], held.at[i], sems.at[i])
        for i in range(count)
    ]
    for copy in copies[:AHEAD]:
        copy.start()
    values, at = [], 0
    table = factors[...]
    for height, rank in shapes:
        values.append(table[at : at + height, :rank])
        at += height
    psi, omega = expand(*values[:2]), expand(*values[2:])
    value = None
    for i in range(count):
        copies[i].wait()
        if i + AHEAD < count:
            copies[i + AHEAD].start()
        block = held[i]
        term = dot(psi[:, i * rows : (i + 1) * rows], block, 1, 0)
        value = term if value is None else value + term
        spans[me[0] ^ i] = dot(omega, block, 1, 1)
    chunk = left.shape[2]
    for c in range(left.shape[0]):
        left[c] = value[:, c * chunk : (c + 1) * chunk]
    part[...] = sum(dot(omega, third, 1, 1) for third in thirds(value))


def sketches(me, snapshots, left_slow, left_fast, right_slow, right_fast, chunk, count):
    height, width = snapshots.shape
    rank_left, rank_right = left_slow.shape[0], right_slow.shape[0]
    factors = [f.T for f in (left_slow, left_fast, right_slow, right_fast)]
    rank = max(rank_left, rank_right)
    table = jnp.concatenate([jnp.pad(f, ((0, 0), (0, rank - f.shape[1]))) for f in factors])
    rows = height // count
    return pl.pallas_call(
        functools.partial(sketch_kernel, [f.shape for f in factors]),
        in_specs=[pl.BlockSpec(memory_space=pltpu.SMEM), VMEM, HBM],
        out_specs=(VMEM,) * 3,
        out_shape=(
            jax.ShapeDtypeStruct((width // chunk, rank_left, chunk), F32),
            jax.ShapeDtypeStruct((rank_right, rank_left), F32),
            jax.ShapeDtypeStruct((count, rank_right, rows), F32),
        ),
        scratch_shapes=[
            pltpu.VMEM((count, rows, width), BF16),
            pltpu.SemaphoreType.DMA((count,)),
        ],
        compiler_params=pltpu.CompilerParams(vmem_limit_bytes=LARGE),
        cost_estimate=pl.CostEstimate(
            flops=2 * (rank_left + rank_right) * height * width,
            bytes_accessed=2 * height * width,
            transcendentals=0,
        ),
        name="sketches",
    )(me, table, snapshots)


def row_of(tile, at):
    return jnp.broadcast_to(tile[at : at + 1, :], tile.shape)


def eliminate(gram):
    size = gram.shape[0]
    lane = lax.broadcasted_iota(jnp.int32, (8, size), 1)
    sub = lax.broadcasted_iota(jnp.int32, (8, size), 0)
    tiles = [gram[i : i + 8] for i in range(0, size, 8)]
    scaled = []
    for t in range(len(tiles)):
        k = 8 * t
        live = range(t, len(tiles))
        column = [
            {i: jnp.broadcast_to(tiles[i][:, k + j : k + j + 1], (8, size)) for i in live}
            for j in range(8)
        ]
        inside = (lane >= k) & (lane < k + 8)
        for i in live:
            tiles[i] = jnp.where(inside, 0.0, tiles[i])
        row = [row_of(tiles[t], j) for j in range(8)]
        weight = [None] * 8
        for p in range(0, 8, 2):
            q = p + 1
            a = row_of(column[p][t], p)
            b = row_of(column[q][t], p)
            c = row_of(column[q][t], q)
            det = a * c - b * b
            inverse = pl.reciprocal(det, approx=True)
            inverse = inverse * (2.0 - det * inverse)
            a, b, c = c * inverse, -b * inverse, a * inverse
            row[p] = jnp.where(lane == k + p, 1.0, row[p])
            row[q] = jnp.where(lane == k + q, 1.0, row[q])
            weight[p] = a * row[p] + b * row[q]
            weight[q] = b * row[p] + c * row[q]
            for j in range(q + 1, 8):
                f, g = row_of(column[j][t], p), row_of(column[j][t], q)
                u, v = a * f + b * g, b * f + c * g
                column[j] = {
                    i: column[j][i] - (column[p][i] * u + column[q][i] * v) for i in live
                }
                row[j] = row[j] - (
                    row_of(column[p][t], j) * weight[p] + row_of(column[q][t], j) * weight[q]
                )
            for i in live[1:]:
                tiles[i] = tiles[i] - (column[p][i] * weight[p] + column[q][i] * weight[q])
        held, out = row[0], weight[0]
        for j in range(1, 8):
            held = jnp.where(sub == j, row[j], held)
            out = jnp.where(sub == j, weight[j], out)
        tiles[t] = held
        scaled.append(out)
    return jnp.concatenate(tiles, 0), jnp.concatenate(scaled, 0)


def factor_kernel(kept, received, side, weight):
    value = (kept[...] + received[...]) * SCALE
    size = value.shape[1]
    i = lax.broadcasted_iota(jnp.int32, (size, size), 0)
    j = lax.broadcasted_iota(jnp.int32, (size, size), 1)
    gram = dot(value, value, 0, 0, HIGHEST) + jnp.where(i == j, RIDGE * SCALE * SCALE, 0.0)
    lower, scaled = eliminate(gram)
    keep = (j >> 1) <= (i >> 1)
    side[...] = dot(value, jnp.where(keep, lower, 0.0), 1, 1, HIGHEST)
    weight[...] = jnp.where(keep, scaled, 0.0) * SCALE


def factor(kept, received):
    size = kept.shape[1]
    return pl.pallas_call(
        factor_kernel,
        out_shape=(
            jax.ShapeDtypeStruct(kept.shape, F32),
            jax.ShapeDtypeStruct((size, size), F32),
        ),
        in_specs=[VMEM, VMEM],
        out_specs=(VMEM, VMEM),
        compiler_params=pltpu.CompilerParams(vmem_limit_bytes=LIMIT),
        cost_estimate=pl.CostEstimate(
            flops=10**10, bytes_accessed=10**5, transcendentals=0
        ),
        name="factor",
    )(kept, received)


def core_kernel(side, weight, kept, received, core):
    left = kept[...] + received[...]
    core[...] = dot(side[...], dot(weight[...], left, 1, 0, HIGHEST), 1, 0, HIGHEST)


def finish(side, weight, kept, received):
    return pl.pallas_call(
        core_kernel,
        out_shape=jax.ShapeDtypeStruct((side.shape[0], kept.shape[1]), F32),
        in_specs=[VMEM] * 4,
        out_specs=VMEM,
        compiler_params=pltpu.CompilerParams(vmem_limit_bytes=LIMIT),
        name="core",
    )(side, weight, kept, received)


def swap(value, axis, size, bit):
    return lax.ppermute(value, axis, [(i, i ^ bit) for i in range(size)])


def bits(size):
    return [1 << b for b in range(size.bit_length() - 1)]


def halve(blocks, axis, size, order):
    count = size.bit_length() - 1
    held = blocks.reshape((2,) * count + blocks.shape[1:])
    me = lax.axis_index(axis)
    dims = bits(size)[::-1]
    kept = received = None
    for bit in order:
        if kept is not None:
            held = kept + received
        dim = dims.index(bit)
        dims.pop(dim)
        mine = (me // bit) % 2
        kept = lax.dynamic_index_in_dim(held, mine, dim, False)
        sent = lax.dynamic_index_in_dim(held, 1 - mine, dim, False)
        received = swap(sent, axis, size, bit)
    return kept, received


def build(sizes):
    cells, samp = sizes["cells"], sizes["samp"]

    def on_device(snapshots, left_slow, left_fast, right_slow, right_fast):
        height, width = snapshots.shape
        share = width // cells
        chunk = share if share % 128 == 0 else width
        me = lax.axis_index("samp").reshape(1)
        chunks, part, spans = sketches(
            me, snapshots, left_slow, left_fast, right_slow, right_fast, chunk, samp
        )
        if chunk != share:
            chunks = chunks[0].reshape(-1, cells, share).transpose(1, 0, 2)

        hops = [("samp", samp, 1), ("cells", cells, 1), ("samp", samp, 2)]
        hops += [("cells", cells, bit) for bit in bits(cells)[1:]]
        received = swap(part, *hops[0])
        for hop in hops[1:]:
            part = part + received
            received = swap(part, *hop)

        crossing = swap(spans[2] + swap(spans[3], "samp", samp, 1), "samp", samp, 2)
        range_part = (spans[0] + swap(spans[1], "samp", samp, 1) + crossing).T

        left_kept, left_received = halve(chunks, "cells", cells, bits(cells))
        side, weight = factor(part, received)
        core = finish(side, weight, left_kept, left_received)
        return (range_part, core)

    return on_device


def solution(mesh):
    placed = (P("cells", "samp"), P(None, "cells"), P(), P(None, "samp"), P())
    return jax.shard_map(
        build(mesh.shape),
        mesh=mesh,
        in_specs=placed,
        out_specs=(P(("cells", "samp"), None), P(None, ("samp", "cells"))),
        check_vma=False,
    )
```

```python
import functools
import math

import jax
import jax.numpy as jnp
from jax import lax
from jax.experimental import pallas as pl
from jax.experimental.pallas import tpu as pltpu
from jax.sharding import PartitionSpec as P

F32 = jnp.float32
BF16 = jnp.bfloat16
HIGHEST = lax.Precision.HIGHEST
SCALE = 2.0**-10
RIDGE = 0.5
COST = 10000
PACE = (0, 0, 10**8, 10**8)
ORDER = "xzyZ"
TIES = {-1: "l", 0: "f", 2: "1", 3: "2", 6: ""}
SPLIT = 1
VMEM = pl.BlockSpec(memory_space=pltpu.VMEM)
HBM = pl.BlockSpec(memory_space=pltpu.HBM)
LIMIT = 16 * 2**20
LARGE = 32 * 2**20
AHEAD = 2


def dot(a, b, a_dim, b_dim, precision=None):
    return lax.dot_general(
        a, b, (((a_dim,), (b_dim,)), ((), ())), precision=precision, preferred_element_type=F32
    )


def repeated(factor_t, width, inner, outer):
    count = factor_t.shape[0]
    row = lax.broadcasted_iota(jnp.int32, (count, width), 0)
    column = lax.broadcasted_iota(jnp.int32, (count, width), 1)
    if outer:
        pick = (column >= row * inner) & (column < (row + 1) * inner)
    elif count & (count - 1) == 0:
        pick = (column & (count - 1)) == row
    else:
        pick = lax.rem(column, count) == row
    return dot(factor_t, jnp.where(pick, 1.0, 0.0).astype(BF16), 0, 0)


def expand(slow_t, fast_t):
    inner = fast_t.shape[0]
    width = slow_t.shape[0] * inner
    period = inner * 128 // math.gcd(inner, 128)
    if width % period:
        period = width
    fast = repeated(fast_t, period, 1, False)
    fast = jnp.concatenate([fast] * (width // period), 1)
    return (repeated(slow_t, width, inner, True) * fast).astype(BF16)


def halves(value):
    high = value.astype(BF16)
    return high, (value - high.astype(F32)).astype(BF16)


def sketch_kernel(place, slow, fast, right_slow, right_fast, slab, left, part, spans, *scratch):
    factors, (held, sems, slab_sems) = scratch[:4], scratch[4:]
    count, rank, rows = spans.shape
    heights = [rows // SPLIT] * (count * SPLIT)
    starts = [i * (rows // SPLIT) for i in range(count * SPLIT)]
    last = len(starts) - 1
    copies = [
        pltpu.make_async_copy(source, target, sems.at[i])
        for i, (source, target) in enumerate(zip((slow, fast, right_slow, right_fast), factors))
    ]
    pieces = [
        pltpu.make_async_copy(slab.at[pl.ds(start, height)], held.at[pl.ds(start, height)], slab_sems.at[i])
        for i, (start, height) in enumerate(zip(starts, heights))
    ]
    for copy in copies:
        copy.start()
    for i, copy in enumerate(pieces[:AHEAD]):
        copy.start(priority=i % 2)
    for copy in copies:
        copy.wait()
    omega = expand(factors[2][...], factors[3][...])
    psi = expand(factors[0][...], factors[1][...])
    value = None
    for i, (start, height) in enumerate(zip(starts, heights)):
        pieces[i].wait()
        if i + AHEAD <= last:
            pieces[i + AHEAD].start(priority=(i + AHEAD) % 2)
        block = held[start : start + height]
        term = dot(psi[:, start : start + height], block, 1, 0)
        value = term if value is None else value + term
        if i == last:
            chunk = left.shape[2]
            for c in range(left.shape[0]):
                left[c] = value[:, c * chunk : (c + 1) * chunk]
            high, low = halves(value)
            whole = dot(omega, high, 1, 1) + dot(omega, low, 1, 1)
            half = part.shape[1]
            bit = place[1]
            part[bit] = whole[:half]
            part[bit ^ 1, : rank - half] = whole[half:]
            part[bit ^ 1, rank - half :] = jnp.zeros((2 * half - rank, whole.shape[1]), F32)
        first = start // rows
        at = start - first * rows
        spans[place[0] ^ first, :, at : at + height] = dot(omega, block, 1, 1)


def half_of(rank):
    return -(-rank // 16) * 8


def sketches(place, snapshots, left_slow, left_fast, right_slow, right_fast, chunk, count):
    height, width = snapshots.shape
    rank_left, rank_right = left_slow.shape[0], right_slow.shape[0]
    factors = [f.T for f in (left_slow, left_fast, right_slow, right_fast)]
    rows = height // count
    inputs = [pltpu.with_memory_space_constraint(x, pltpu.HBM) for x in factors + [snapshots]]
    return pl.pallas_call(
        sketch_kernel,
        in_specs=[pl.BlockSpec(memory_space=pltpu.SMEM)] + [HBM] * 5,
        out_specs=(VMEM,) * 3,
        out_shape=(
            jax.ShapeDtypeStruct((width // chunk, rank_left, chunk), F32),
            jax.ShapeDtypeStruct((2, half_of(rank_right), rank_left), F32),
            jax.ShapeDtypeStruct((count, rank_right, rows), F32),
        ),
        scratch_shapes=[pltpu.VMEM(f.shape, BF16) for f in factors]
        + [
            pltpu.VMEM(snapshots.shape, BF16),
            pltpu.SemaphoreType.DMA((4,)),
            pltpu.SemaphoreType.DMA((count * SPLIT,)),
        ],
        compiler_params=pltpu.CompilerParams(vmem_limit_bytes=LIMIT),
        cost_estimate=pl.CostEstimate(
            flops=2 * (rank_left + rank_right) * height * width,
            bytes_accessed=2 * height * width,
            transcendentals=0,
        ),
        name="sketches",
    )(place, *inputs)


def row_of(tile, at):
    return jnp.broadcast_to(tile[at : at + 1, :], tile.shape)


def eliminate(gram):
    size = gram.shape[0]
    lane = lax.broadcasted_iota(jnp.int32, (8, size), 1)
    sub = lax.broadcasted_iota(jnp.int32, (8, size), 0)
    tiles = [gram[i : i + 8] for i in range(0, size, 8)]
    scaled = []
    for t in range(len(tiles)):
        k = 8 * t
        live = range(t, len(tiles))
        column = [
            {i: jnp.broadcast_to(tiles[i][:, k + j : k + j + 1], (8, size)) for i in live}
            for j in range(8)
        ]
        inside = (lane >= k) & (lane < k + 8)
        for i in live:
            tiles[i] = jnp.where(inside, 0.0, tiles[i])
        row = [row_of(tiles[t], j) for j in range(8)]
        weight = [None] * 8
        for p in range(0, 8, 2):
            q = p + 1
            a = row_of(column[p][t], p)
            b = row_of(column[q][t], p)
            c = row_of(column[q][t], q)
            det = a * c - b * b
            inverse = pl.reciprocal(det, approx=True)
            a, b, c = c * inverse, -b * inverse, a * inverse
            row[p] = jnp.where(lane == k + p, 1.0, row[p])
            row[q] = jnp.where(lane == k + q, 1.0, row[q])
            weight[p] = a * row[p] + b * row[q]
            weight[q] = b * row[p] + c * row[q]
            for j in range(q + 1, 8):
                f, g = row_of(column[j][t], p), row_of(column[j][t], q)
                u, v = a * f + b * g, b * f + c * g
                column[j] = {
                    i: column[j][i] - (column[p][i] * u + column[q][i] * v) for i in live
                }
                row[j] = row[j] - (
                    row_of(column[p][t], j) * weight[p] + row_of(column[q][t], j) * weight[q]
                )
            for i in live[1:]:
                tiles[i] = tiles[i] - (column[p][i] * weight[p] + column[q][i] * weight[q])
        held, out = row[0], weight[0]
        for j in range(1, 8):
            held = jnp.where(sub == j, row[j], held)
            out = jnp.where(sub == j, weight[j], out)
        tiles[t] = held
        scaled.append(out)
    return jnp.concatenate(tiles, 0), jnp.concatenate(scaled, 0)


def factor_kernel(low_first, mine, other, side, weight):
    first = low_first[0] == 0
    mine, other = mine[...], other[...]
    half = mine.shape[0]
    low, high = jnp.where(first, mine, other), jnp.where(first, other, mine)
    value = jnp.concatenate([low, high[: side.shape[0] - half]], 0) * SCALE
    size = value.shape[1]
    i = lax.broadcasted_iota(jnp.int32, (size, size), 0)
    j = lax.broadcasted_iota(jnp.int32, (size, size), 1)
    gram = dot(value, value, 0, 0, HIGHEST) + jnp.where(i == j, RIDGE * SCALE * SCALE, 0.0)
    lower, scaled = eliminate(gram)
    keep = (j >> 1) <= (i >> 1)
    side[...] = dot(value, jnp.where(keep, lower, 0.0), 1, 1, HIGHEST)
    weight[...] = jnp.where(keep, scaled, 0.0) * SCALE


def factor(low_first, mine, other, rank):
    size = mine.shape[1]
    return pl.pallas_call(
        factor_kernel,
        out_shape=(
            jax.ShapeDtypeStruct((rank, size), F32),
            jax.ShapeDtypeStruct((size, size), F32),
        ),
        in_specs=[pl.BlockSpec(memory_space=pltpu.SMEM)] + [VMEM] * 2,
        out_specs=(VMEM, VMEM),
        compiler_params=pltpu.CompilerParams(vmem_limit_bytes=LIMIT),
        cost_estimate=pl.CostEstimate(flops=COST, bytes_accessed=1000, transcendentals=0),
        name="factor",
    )(low_first, mine, other)


def pass_on(*refs):
    del refs


def paced(value, pace):
    if not pace:
        return value
    anywhere = pl.BlockSpec(memory_space=pl.ANY)
    return pl.pallas_call(
        pass_on,
        out_shape=jax.ShapeDtypeStruct(value.shape, value.dtype),
        in_specs=[anywhere],
        out_specs=anywhere,
        input_output_aliases={0: 0},
        compiler_params=pltpu.CompilerParams(vmem_limit_bytes=LIMIT),
        cost_estimate=pl.CostEstimate(flops=pace, bytes_accessed=0, transcendentals=0),
        name="paced",
    )(value)


def core_kernel(side, weight, kept, received, core):
    left = kept[...] + received[...]
    core[...] = dot(side[...], dot(weight[...], left, 1, 0, HIGHEST), 1, 0, HIGHEST)


def finish(side, weight, kept, received):
    return pl.pallas_call(
        core_kernel,
        out_shape=jax.ShapeDtypeStruct((side.shape[0], kept.shape[1]), F32),
        in_specs=[VMEM] * 4,
        out_specs=VMEM,
        compiler_params=pltpu.CompilerParams(vmem_limit_bytes=LIMIT),
        name="core",
    )(side, weight, kept, received)


def swap(value, axis, size, bit):
    return lax.ppermute(value, axis, [(i, i ^ bit) for i in range(size)])


def across(value, sizes, cell_bit, samp_bit):
    cells, samp = sizes
    pairs = [
        (i * samp + j, (i ^ cell_bit) * samp + (j ^ samp_bit ^ 1))
        for i in range(cells)
        for j in range(samp)
    ]
    return lax.ppermute(value, ("cells", "samp"), pairs)


def bits(size):
    return [1 << b for b in range(size.bit_length() - 1)]


def side_of(blocks, axis, bit, dim):
    mine = (lax.axis_index(axis) // bit) % 2
    return (
        lax.dynamic_index_in_dim(blocks, mine, dim, False),
        lax.dynamic_index_in_dim(blocks, 1 - mine, dim, False),
    )


def halving(blocks, axis, size, bit, dim):
    kept, sent = side_of(blocks, axis, bit, dim)
    return kept, swap(sent, axis, size, bit)


def build(sizes):
    cells, samp = sizes["cells"], sizes["samp"]

    def on_device(snapshots, left_slow, left_fast, right_slow, right_fast):
        height, width = snapshots.shape
        share = width // cells
        chunk = share if share % 128 == 0 else width
        me, cell = lax.axis_index("samp"), lax.axis_index("cells")
        flips = [me >> b for b in range(len(bits(samp)))] + [cell >> b for b in range(len(bits(cells)))]
        half = functools.reduce(lax.bitwise_xor, flips) & 1
        chunks, part, spans = sketches(
            jnp.stack([me, half]), snapshots, left_slow, left_fast, right_slow, right_fast, chunk, samp
        )
        if chunk != share:
            chunks = chunks[0].reshape(-1, cells, share).transpose(1, 0, 2)

        together = lax.optimization_barrier
        levels = bits(cells)
        left = chunks.reshape((2,) * len(levels) + chunks.shape[1:])

        sizes = (cells, samp)
        dims = levels[::-1]
        bit_of = {"y": levels[0], "z": levels[1], "Z": levels[2], "x": 2}
        far = spans[3] + swap(spans[2], "samp", samp, 1)
        near = (spans[0], swap(spans[1], "samp", samp, 1))
        now = {"l": left, "f": far}

        def tie(step, mine):
            for name in TIES.get(step, ""):
                if name in now:
                    mine, now[name] = together((mine, now[name]))
                if name == "f":
                    now["c"] = swap(now["f"], "samp", samp, 3)
                if name == "l" and True:
                    now["h1"] = halving(now["l"], "cells", cells, levels[0], len(levels) - 1)
                    now["1"] = sum(now["h1"])
                if False:
                    stay, leave = side_of(now["l"], "cells", levels[1], len(levels) - 2)
                    now["1"] = sum(halving(leave, "cells", cells, levels[0], len(levels) - 2))
                    now["s"] = sum(halving(stay, "cells", cells, levels[0], len(levels) - 2))
                if name == "1" and True:
                    now["h2"] = halving(now["1"], "cells", cells, levels[1], len(levels) - 2)
                    now["2"] = sum(now["h2"])
                if False:
                    now["2"] = now["s"] + swap(now["1"], "cells", cells, levels[1])
                if name == "2":
                    dim3 = len(levels) - 3
                    now["h3"] = halving(now["2"], "cells", cells, levels[2], len(levels) - 3)
            return mine

        part = tie(-1, part)
        mine = tie(0, part[0] + swap(part[1], "samp", samp, 1))
        for step, letter in enumerate(ORDER):
            if letter == "x":
                mine = mine + across(mine, sizes, 0, 2)
            else:
                mine = mine + across(mine, sizes, bit_of[letter], 0)
            mine = tie(step + 1, paced(mine, PACE[step]))
        for bit in levels[3:]:
            mine = mine + across(mine, sizes, bit, 0)
        other = swap(mine, "samp", samp, 1)
        tie(5, mine)
        if "1" in now and "2" not in now:
            tie_free = halving(now["1"], "cells", cells, levels[1], len(levels) - 2)
            now["2"] = sum(tie_free)
        if "h3" not in now:
            now["h3"] = halving(now["2"], "cells", cells, levels[2], len(levels) - 3)
        range_part = near[0] + near[1] + now["c"]
        if 6 in TIES:
            other, range_part = together((other, range_part))
        rest = now["h3"]
        for step, bit in enumerate(levels[3:]):
            rest = halving(sum(rest), "cells", cells, bit, len(levels) - 4 - step)
        if 7 in TIES:
            other, got = together((other, rest[1]))
            rest = (rest[0], got)
        side, weight = factor(half.reshape(1), mine, other, right_slow.shape[0])
        return (range_part.T, finish(side, weight, *rest))

    return on_device


def solution(mesh):
    placed = (P("cells", "samp"), P(None, "cells"), P(), P(None, "samp"), P())
    return jax.shard_map(
        build(mesh.shape),
        mesh=mesh,
        in_specs=placed,
        out_specs=(P(("cells", "samp"), None), P(None, ("samp", "cells"))),
        check_vma=False,
    )
```

```python
import functools
import math

import jax
import jax.numpy as jnp
from jax import lax
from jax.experimental import pallas as pl
from jax.experimental.pallas import tpu as pltpu
from jax.sharding import PartitionSpec as P

F32 = jnp.float32
BF16 = jnp.bfloat16
HIGHEST = lax.Precision.HIGHEST
SCALE = 2.0**-10
RIDGE = 0.5
COST = 10000
PACE = (0, 0, 10**8, 10**8)
ORDER = "xzyZ"
TIES = {-1: "l", 0: "fg", 2: "1", 3: "2", 6: ""}
SPLIT = 1
VMEM = pl.BlockSpec(memory_space=pltpu.VMEM)
HBM = pl.BlockSpec(memory_space=pltpu.HBM)
LIMIT = 16 * 2**20
LARGE = 32 * 2**20
AHEAD = 2


def dot(a, b, a_dim, b_dim, precision=None):
    return lax.dot_general(
        a, b, (((a_dim,), (b_dim,)), ((), ())), precision=precision, preferred_element_type=F32
    )


def repeated(factor_t, width, inner, outer):
    count = factor_t.shape[0]
    row = lax.broadcasted_iota(jnp.int32, (count, width), 0)
    column = lax.broadcasted_iota(jnp.int32, (count, width), 1)
    if outer:
        pick = (column >= row * inner) & (column < (row + 1) * inner)
    elif count & (count - 1) == 0:
        pick = (column & (count - 1)) == row
    else:
        pick = lax.rem(column, count) == row
    return dot(factor_t, jnp.where(pick, 1.0, 0.0).astype(BF16), 0, 0)


def expand(slow_t, fast_t):
    inner = fast_t.shape[0]
    width = slow_t.shape[0] * inner
    period = inner * 128 // math.gcd(inner, 128)
    if width % period:
        period = width
    fast = repeated(fast_t, period, 1, False)
    fast = jnp.concatenate([fast] * (width // period), 1)
    return (repeated(slow_t, width, inner, True) * fast).astype(BF16)


def halves(value):
    high = value.astype(BF16)
    return high, (value - high.astype(F32)).astype(BF16)


def sketch_kernel(place, slow, fast, right_slow, right_fast, slab, left, part, spans, *scratch):
    factors, (held, sems, slab_sems) = scratch[:4], scratch[4:]
    count, rank, rows = spans.shape
    heights = [rows // SPLIT] * (count * SPLIT)
    starts = [i * (rows // SPLIT) for i in range(count * SPLIT)]
    last = len(starts) - 1
    copies = [
        pltpu.make_async_copy(source, target, sems.at[i])
        for i, (source, target) in enumerate(zip((slow, fast, right_slow, right_fast), factors))
    ]
    pieces = [
        pltpu.make_async_copy(slab.at[pl.ds(start, height)], held.at[pl.ds(start, height)], slab_sems.at[i])
        for i, (start, height) in enumerate(zip(starts, heights))
    ]
    for copy in copies:
        copy.start()
    for i, copy in enumerate(pieces[:AHEAD]):
        copy.start(priority=i % 2)
    for copy in copies:
        copy.wait()
    omega = expand(factors[2][...], factors[3][...])
    psi = expand(factors[0][...], factors[1][...])
    value = None
    for i, (start, height) in enumerate(zip(starts, heights)):
        pieces[i].wait()
        if i + AHEAD <= last:
            pieces[i + AHEAD].start(priority=(i + AHEAD) % 2)
        block = held[start : start + height]
        term = dot(psi[:, start : start + height], block, 1, 0)
        value = term if value is None else value + term
        if i == last:
            chunk = left.shape[2]
            for c in range(left.shape[0]):
                left[c] = value[:, c * chunk : (c + 1) * chunk]
            high, low = halves(value)
            whole = dot(omega, high, 1, 1) + dot(omega, low, 1, 1)
            half = part.shape[1]
            bit = place[1]
            part[bit] = whole[:half]
            part[bit ^ 1, : rank - half] = whole[half:]
            part[bit ^ 1, rank - half :] = jnp.zeros((2 * half - rank, whole.shape[1]), F32)
        first = start // rows
        at = start - first * rows
        spans[place[0] ^ first, :, at : at + height] = dot(omega, block, 1, 1)


def half_of(rank):
    return -(-rank // 16) * 8


def sketches(place, snapshots, left_slow, left_fast, right_slow, right_fast, chunk, count):
    height, width = snapshots.shape
    rank_left, rank_right = left_slow.shape[0], right_slow.shape[0]
    factors = [f.T for f in (left_slow, left_fast, right_slow, right_fast)]
    rows = height // count
    inputs = [pltpu.with_memory_space_constraint(x, pltpu.HBM) for x in factors + [snapshots]]
    return pl.pallas_call(
        sketch_kernel,
        in_specs=[pl.BlockSpec(memory_space=pltpu.SMEM)] + [HBM] * 5,
        out_specs=(VMEM,) * 3,
        out_shape=(
            jax.ShapeDtypeStruct((width // chunk, rank_left, chunk), F32),
            jax.ShapeDtypeStruct((2, half_of(rank_right), rank_left), F32),
            jax.ShapeDtypeStruct((count, rank_right, rows), F32),
        ),
        scratch_shapes=[pltpu.VMEM(f.shape, BF16) for f in factors]
        + [
            pltpu.VMEM(snapshots.shape, BF16),
            pltpu.SemaphoreType.DMA((4,)),
            pltpu.SemaphoreType.DMA((count * SPLIT,)),
        ],
        compiler_params=pltpu.CompilerParams(vmem_limit_bytes=LIMIT),
        cost_estimate=pl.CostEstimate(
            flops=2 * (rank_left + rank_right) * height * width,
            bytes_accessed=2 * height * width,
            transcendentals=0,
        ),
        name="sketches",
    )(place, *inputs)


def row_of(tile, at):
    return jnp.broadcast_to(tile[at : at + 1, :], tile.shape)


def eliminate(gram):
    size = gram.shape[0]
    lane = lax.broadcasted_iota(jnp.int32, (8, size), 1)
    sub = lax.broadcasted_iota(jnp.int32, (8, size), 0)
    tiles = [gram[i : i + 8] for i in range(0, size, 8)]
    scaled = []
    for t in range(len(tiles)):
        k = 8 * t
        live = range(t, len(tiles))
        column = [
            {i: jnp.broadcast_to(tiles[i][:, k + j : k + j + 1], (8, size)) for i in live}
            for j in range(8)
        ]
        inside = (lane >= k) & (lane < k + 8)
        for i in live:
            tiles[i] = jnp.where(inside, 0.0, tiles[i])
        row = [row_of(tiles[t], j) for j in range(8)]
        weight = [None] * 8
        for p in range(0, 8, 2):
            q = p + 1
            a = row_of(column[p][t], p)
            b = row_of(column[q][t], p)
            c = row_of(column[q][t], q)
            det = a * c - b * b
            inverse = pl.reciprocal(det, approx=True)
            a, b, c = c * inverse, -b * inverse, a * inverse
            row[p] = jnp.where(lane == k + p, 1.0, row[p])
            row[q] = jnp.where(lane == k + q, 1.0, row[q])
            weight[p] = a * row[p] + b * row[q]
            weight[q] = b * row[p] + c * row[q]
            for j in range(q + 1, 8):
                f, g = row_of(column[j][t], p), row_of(column[j][t], q)
                u, v = a * f + b * g, b * f + c * g
                column[j] = {
                    i: column[j][i] - (column[p][i] * u + column[q][i] * v) for i in live
                }
                row[j] = row[j] - (
                    row_of(column[p][t], j) * weight[p] + row_of(column[q][t], j) * weight[q]
                )
            for i in live[1:]:
                tiles[i] = tiles[i] - (column[p][i] * weight[p] + column[q][i] * weight[q])
        held, out = row[0], weight[0]
        for j in range(1, 8):
            held = jnp.where(sub == j, row[j], held)
            out = jnp.where(sub == j, weight[j], out)
        tiles[t] = held
        scaled.append(out)
    return jnp.concatenate(tiles, 0), jnp.concatenate(scaled, 0)


def factor_kernel(low_first, mine, other, side, weight):
    first = low_first[0] == 0
    mine, other = mine[...], other[...]
    half = mine.shape[0]
    low, high = jnp.where(first, mine, other), jnp.where(first, other, mine)
    value = jnp.concatenate([low, high[: side.shape[0] - half]], 0) * SCALE
    size = value.shape[1]
    i = lax.broadcasted_iota(jnp.int32, (size, size), 0)
    j = lax.broadcasted_iota(jnp.int32, (size, size), 1)
    gram = dot(value, value, 0, 0, HIGHEST) + jnp.where(i == j, RIDGE * SCALE * SCALE, 0.0)
    lower, scaled = eliminate(gram)
    keep = (j >> 1) <= (i >> 1)
    side[...] = dot3(value, jnp.where(keep, lower, 0.0), 1, 1)
    weight[...] = jnp.where(keep, scaled, 0.0) * SCALE


def factor(low_first, mine, other, rank):
    size = mine.shape[1]
    return pl.pallas_call(
        factor_kernel,
        out_shape=(
            jax.ShapeDtypeStruct((rank, size), F32),
            jax.ShapeDtypeStruct((size, size), F32),
        ),
        in_specs=[pl.BlockSpec(memory_space=pltpu.SMEM)] + [VMEM] * 2,
        out_specs=(VMEM, VMEM),
        compiler_params=pltpu.CompilerParams(vmem_limit_bytes=LIMIT),
        cost_estimate=pl.CostEstimate(flops=COST, bytes_accessed=1000, transcendentals=0),
        name="factor",
    )(low_first, mine, other)


def pass_on(*refs):
    del refs


def paced(value, pace):
    if not pace:
        return value
    anywhere = pl.BlockSpec(memory_space=pl.ANY)
    return pl.pallas_call(
        pass_on,
        out_shape=jax.ShapeDtypeStruct(value.shape, value.dtype),
        in_specs=[anywhere],
        out_specs=anywhere,
        input_output_aliases={0: 0},
        compiler_params=pltpu.CompilerParams(vmem_limit_bytes=LIMIT),
        cost_estimate=pl.CostEstimate(flops=pace, bytes_accessed=0, transcendentals=0),
        name="paced",
    )(value)


def dot3(a, b, a_dim, b_dim):
    (a_high, a_low), (b_high, b_low) = halves(a), halves(b)
    small = dot(a_high, b_low, a_dim, b_dim) + dot(a_low, b_high, a_dim, b_dim)
    return dot(a_high, b_high, a_dim, b_dim) + small


def core_kernel(side, weight, kept, received, core):
    left = kept[...] + received[...]
    core[...] = dot3(side[...], dot3(weight[...], left, 1, 0), 1, 0)


def finish(side, weight, kept, received):
    return pl.pallas_call(
        core_kernel,
        out_shape=jax.ShapeDtypeStruct((side.shape[0], kept.shape[1]), F32),
        in_specs=[VMEM] * 4,
        out_specs=VMEM,
        compiler_params=pltpu.CompilerParams(vmem_limit_bytes=LIMIT),
        name="core",
    )(side, weight, kept, received)


def swap(value, axis, size, bit):
    return lax.ppermute(value, axis, [(i, i ^ bit) for i in range(size)])


def across(value, sizes, cell_bit, samp_bit):
    cells, samp = sizes
    pairs = [
        (i * samp + j, (i ^ cell_bit) * samp + (j ^ samp_bit ^ 1))
        for i in range(cells)
        for j in range(samp)
    ]
    return lax.ppermute(value, ("cells", "samp"), pairs)


def bits(size):
    return [1 << b for b in range(size.bit_length() - 1)]


def side_of(blocks, axis, bit, dim):
    mine = (lax.axis_index(axis) // bit) % 2
    return (
        lax.dynamic_index_in_dim(blocks, mine, dim, False),
        lax.dynamic_index_in_dim(blocks, 1 - mine, dim, False),
    )


def halving(blocks, axis, size, bit, dim):
    kept, sent = side_of(blocks, axis, bit, dim)
    return kept, swap(sent, axis, size, bit)


def build(sizes):
    cells, samp = sizes["cells"], sizes["samp"]

    def on_device(snapshots, left_slow, left_fast, right_slow, right_fast):
        height, width = snapshots.shape
        share = width // cells
        chunk = share if share % 128 == 0 else width
        me, cell = lax.axis_index("samp"), lax.axis_index("cells")
        flips = [me >> b for b in range(len(bits(samp)))] + [cell >> b for b in range(len(bits(cells)))]
        half = functools.reduce(lax.bitwise_xor, flips) & 1
        chunks, part, spans = sketches(
            jnp.stack([me, half]), snapshots, left_slow, left_fast, right_slow, right_fast, chunk, samp
        )
        if chunk != share:
            chunks = chunks[0].reshape(-1, cells, share).transpose(1, 0, 2)

        together = lax.optimization_barrier
        levels = bits(cells)
        left = chunks.reshape((2,) * len(levels) + chunks.shape[1:])

        sizes = (cells, samp)
        dims = levels[::-1]
        bit_of = {"y": levels[0], "z": levels[1], "Z": levels[2], "x": 2}
        far = spans[3] + swap(spans[2], "samp", samp, 1)
        near = (spans[0], swap(spans[1], "samp", samp, 1))
        now = {"l": left, "f": far}

        def tie(step, mine):
            for name in TIES.get(step, ""):
                if name in now:
                    mine, now[name] = together((mine, now[name]))
                if name == "g":
                    mine, now["f"] = together((mine, now["f"]))
                    now["c"] = swap(now["f"], "samp", samp, 3)
                if name == "l" and True:
                    now["h1"] = halving(now["l"], "cells", cells, levels[0], len(levels) - 1)
                    now["1"] = sum(now["h1"])
                if False:
                    stay, leave = side_of(now["l"], "cells", levels[1], len(levels) - 2)
                    now["1"] = sum(halving(leave, "cells", cells, levels[0], len(levels) - 2))
                    now["s"] = sum(halving(stay, "cells", cells, levels[0], len(levels) - 2))
                if name == "1" and True:
                    now["h2"] = halving(now["1"], "cells", cells, levels[1], len(levels) - 2)
                    now["2"] = sum(now["h2"])
                if False:
                    now["2"] = now["s"] + swap(now["1"], "cells", cells, levels[1])
                if name == "2":
                    dim3 = len(levels) - 3
                    now["h3"] = halving(now["2"], "cells", cells, levels[2], len(levels) - 3)
            return mine

        part = tie(-1, part)
        mine = tie(0, part[0] + swap(part[1], "samp", samp, 1))
        for step, letter in enumerate(ORDER):
            if letter == "x":
                mine = mine + across(mine, sizes, 0, 2)
            else:
                mine = mine + across(mine, sizes, bit_of[letter], 0)
            mine = tie(step + 1, paced(mine, PACE[step]))
        for bit in levels[3:]:
            mine = mine + across(mine, sizes, bit, 0)
        other = swap(mine, "samp", samp, 1)
        tie(5, mine)
        if "1" in now and "2" not in now:
            tie_free = halving(now["1"], "cells", cells, levels[1], len(levels) - 2)
            now["2"] = sum(tie_free)
        if "h3" not in now:
            now["h3"] = halving(now["2"], "cells", cells, levels[2], len(levels) - 3)
        range_part = near[0] + near[1] + now["c"]
        if 6 in TIES:
            other, range_part = together((other, range_part))
        rest = now["h3"]
        for step, bit in enumerate(levels[3:]):
            rest = halving(sum(rest), "cells", cells, bit, len(levels) - 4 - step)
        if 7 in TIES:
            other, got = together((other, rest[1]))
            rest = (rest[0], got)
        side, weight = factor(half.reshape(1), mine, other, right_slow.shape[0])
        return (range_part.T, finish(side, weight, *rest))

    return on_device


def solution(mesh):
    placed = (P("cells", "samp"), P(None, "cells"), P(), P(None, "samp"), P())
    return jax.shard_map(
        build(mesh.shape),
        mesh=mesh,
        in_specs=placed,
        out_specs=(P(("cells", "samp"), None), P(None, ("samp", "cells"))),
        check_vma=False,
    )
```

```python
import functools
import math

import jax
import jax.numpy as jnp
from jax import lax
from jax.experimental import pallas as pl
from jax.experimental.pallas import tpu as pltpu
from jax.sharding import PartitionSpec as P

F32 = jnp.float32
BF16 = jnp.bfloat16
HIGHEST = lax.Precision.HIGHEST
SCALE = 2.0**-10
RIDGE = 0.5
VMEM = pl.BlockSpec(memory_space=pltpu.VMEM)
HBM = pl.BlockSpec(memory_space=pltpu.HBM)
LIMIT = 16 * 2**20
AHEAD = 2


def dot(a, b, a_dim, b_dim, precision=None):
    return lax.dot_general(
        a, b, (((a_dim,), (b_dim,)), ((), ())), precision=precision, preferred_element_type=F32
    )


def repeated(factor_t, width, inner, outer):
    count = factor_t.shape[0]
    row = lax.broadcasted_iota(jnp.int32, (count, width), 0)
    column = lax.broadcasted_iota(jnp.int32, (count, width), 1)
    if outer:
        pick = (column >= row * inner) & (column < (row + 1) * inner)
    elif count & (count - 1) == 0:
        pick = (column & (count - 1)) == row
    else:
        pick = lax.rem(column, count) == row
    return dot(factor_t, jnp.where(pick, 1.0, 0.0).astype(BF16), 0, 0)


def expand(slow_t, fast_t):
    inner = fast_t.shape[0]
    width = slow_t.shape[0] * inner
    period = inner * 128 // math.gcd(inner, 128)
    if width % period:
        period = width
    fast = repeated(fast_t, period, 1, False)
    fast = jnp.concatenate([fast] * (width // period), 1)
    return (repeated(slow_t, width, inner, True) * fast).astype(BF16)


def halves(value):
    high = value.astype(BF16)
    return high, (value - high.astype(F32)).astype(BF16)


def sketch_kernel(place, slow, fast, right_slow, right_fast, slab, left, part, spans, *scratch):
    factors, (held, sems, slab_sems) = scratch[:4], scratch[4:]
    count, rank, rows = spans.shape
    starts = [i * rows for i in range(count)]
    copies = [
        pltpu.make_async_copy(source, target, sems.at[i])
        for i, (source, target) in enumerate(zip((slow, fast, right_slow, right_fast), factors))
    ]
    pieces = [
        pltpu.make_async_copy(slab.at[pl.ds(start, rows)], held.at[pl.ds(start, rows)], slab_sems.at[i])
        for i, start in enumerate(starts)
    ]
    for copy in copies:
        copy.start()
    for i, copy in enumerate(pieces[:AHEAD]):
        copy.start(priority=i % 2)
    for copy in copies:
        copy.wait()
    omega = expand(factors[2][...], factors[3][...])
    psi = expand(factors[0][...], factors[1][...])
    value = None
    for i, start in enumerate(starts):
        pieces[i].wait()
        if i + AHEAD < count:
            pieces[i + AHEAD].start(priority=(i + AHEAD) % 2)
        block = held[start : start + rows]
        term = dot(psi[:, start : start + rows], block, 1, 0)
        value = term if value is None else value + term
        if i == count - 1:
            chunk = left.shape[2]
            for c in range(left.shape[0]):
                left[c] = value[:, c * chunk : (c + 1) * chunk]
            high, low = halves(value)
            whole = dot(omega, high, 1, 1) + dot(omega, low, 1, 1)
            half = part.shape[1]
            bit = place[1]
            part[bit] = whole[:half]
            part[bit ^ 1, : rank - half] = whole[half:]
            part[bit ^ 1, rank - half :] = jnp.zeros((2 * half - rank, whole.shape[1]), F32)
        spans[place[0] ^ i] = dot(omega, block, 1, 1)


def half_of(rank):
    return -(-rank // 16) * 8


def sketches(place, snapshots, left_slow, left_fast, right_slow, right_fast, chunk, count):
    height, width = snapshots.shape
    rank_left, rank_right = left_slow.shape[0], right_slow.shape[0]
    factors = [f.T for f in (left_slow, left_fast, right_slow, right_fast)]
    rows = height // count
    inputs = [pltpu.with_memory_space_constraint(x, pltpu.HBM) for x in factors + [snapshots]]
    return pl.pallas_call(
        sketch_kernel,
        in_specs=[pl.BlockSpec(memory_space=pltpu.SMEM)] + [HBM] * 5,
        out_specs=(VMEM,) * 3,
        out_shape=(
            jax.ShapeDtypeStruct((width // chunk, rank_left, chunk), F32),
            jax.ShapeDtypeStruct((2, half_of(rank_right), rank_left), F32),
            jax.ShapeDtypeStruct((count, rank_right, rows), F32),
        ),
        scratch_shapes=[pltpu.VMEM(f.shape, BF16) for f in factors]
        + [
            pltpu.VMEM(snapshots.shape, BF16),
            pltpu.SemaphoreType.DMA((4,)),
            pltpu.SemaphoreType.DMA((count,)),
        ],
        compiler_params=pltpu.CompilerParams(vmem_limit_bytes=LIMIT),
        cost_estimate=pl.CostEstimate(
            flops=2 * (rank_left + rank_right) * height * width,
            bytes_accessed=2 * height * width,
            transcendentals=0,
        ),
        name="sketches",
    )(place, *inputs)


def row_of(tile, at):
    return jnp.broadcast_to(tile[at : at + 1, :], tile.shape)


def eliminate(gram):
    size = gram.shape[0]
    lane = lax.broadcasted_iota(jnp.int32, (8, size), 1)
    sub = lax.broadcasted_iota(jnp.int32, (8, size), 0)
    tiles = [gram[i : i + 8] for i in range(0, size, 8)]
    scaled = []
    for t in range(len(tiles)):
        k = 8 * t
        live = range(t, len(tiles))
        column = [
            {i: jnp.broadcast_to(tiles[i][:, k + j : k + j + 1], (8, size)) for i in live}
            for j in range(8)
        ]
        inside = (lane >= k) & (lane < k + 8)
        for i in live:
            tiles[i] = jnp.where(inside, 0.0, tiles[i])
        row = [row_of(tiles[t], j) for j in range(8)]
        weight = [None] * 8
        for p in range(0, 8, 2):
            q = p + 1
            a = row_of(column[p][t], p)
            b = row_of(column[q][t], p)
            c = row_of(column[q][t], q)
            det = a * c - b * b
            inverse = pl.reciprocal(det, approx=True)
            a, b, c = c * inverse, -b * inverse, a * inverse
            row[p] = jnp.where(lane == k + p, 1.0, row[p])
            row[q] = jnp.where(lane == k + q, 1.0, row[q])
            weight[p] = a * row[p] + b * row[q]
            weight[q] = b * row[p] + c * row[q]
            for j in range(q + 1, 8):
                f, g = row_of(column[j][t], p), row_of(column[j][t], q)
                u, v = a * f + b * g, b * f + c * g
                column[j] = {
                    i: column[j][i] - (column[p][i] * u + column[q][i] * v) for i in live
                }
                row[j] = row[j] - (
                    row_of(column[p][t], j) * weight[p] + row_of(column[q][t], j) * weight[q]
                )
            for i in live[1:]:
                tiles[i] = tiles[i] - (column[p][i] * weight[p] + column[q][i] * weight[q])
        held, out = row[0], weight[0]
        for j in range(1, 8):
            held = jnp.where(sub == j, row[j], held)
            out = jnp.where(sub == j, weight[j], out)
        tiles[t] = held
        scaled.append(out)
    return jnp.concatenate(tiles, 0), jnp.concatenate(scaled, 0)


def factor_kernel(low_first, mine, other, side, weight):
    first = low_first[0] == 0
    mine, other = mine[...], other[...]
    half = mine.shape[0]
    low, high = jnp.where(first, mine, other), jnp.where(first, other, mine)
    value = jnp.concatenate([low, high[: side.shape[0] - half]], 0) * SCALE
    size = value.shape[1]
    i = lax.broadcasted_iota(jnp.int32, (size, size), 0)
    j = lax.broadcasted_iota(jnp.int32, (size, size), 1)
    gram = dot(value, value, 0, 0, HIGHEST) + jnp.where(i == j, RIDGE * SCALE * SCALE, 0.0)
    lower, scaled = eliminate(gram)
    keep = (j >> 1) <= (i >> 1)
    side[...] = dot3(value, jnp.where(keep, lower, 0.0), 1, 1)
    weight[...] = jnp.where(keep, scaled, 0.0) * SCALE


def factor(low_first, mine, other, rank):
    size = mine.shape[1]
    return pl.pallas_call(
        factor_kernel,
        out_shape=(
            jax.ShapeDtypeStruct((rank, size), F32),
            jax.ShapeDtypeStruct((size, size), F32),
        ),
        in_specs=[pl.BlockSpec(memory_space=pltpu.SMEM)] + [VMEM] * 2,
        out_specs=(VMEM, VMEM),
        compiler_params=pltpu.CompilerParams(vmem_limit_bytes=LIMIT),
        cost_estimate=pl.CostEstimate(flops=10**4, bytes_accessed=1000, transcendentals=0),
        name="factor",
    )(low_first, mine, other)


def pass_on(*refs):
    del refs


def paced(value, pace):
    anywhere = pl.BlockSpec(memory_space=pl.ANY)
    return pl.pallas_call(
        pass_on,
        out_shape=jax.ShapeDtypeStruct(value.shape, value.dtype),
        in_specs=[anywhere],
        out_specs=anywhere,
        input_output_aliases={0: 0},
        compiler_params=pltpu.CompilerParams(vmem_limit_bytes=LIMIT),
        cost_estimate=pl.CostEstimate(flops=pace, bytes_accessed=0, transcendentals=0),
        name="paced",
    )(value)


def dot3(a, b, a_dim, b_dim):
    (a_high, a_low), (b_high, b_low) = halves(a), halves(b)
    small = dot(a_high, b_low, a_dim, b_dim) + dot(a_low, b_high, a_dim, b_dim)
    return dot(a_high, b_high, a_dim, b_dim) + small


def core_kernel(side, weight, kept, received, core):
    left = kept[...] + received[...]
    core[...] = dot3(side[...], dot3(weight[...], left, 1, 0), 1, 0)


def finish(side, weight, kept, received):
    return pl.pallas_call(
        core_kernel,
        out_shape=jax.ShapeDtypeStruct((side.shape[0], kept.shape[1]), F32),
        in_specs=[VMEM] * 4,
        out_specs=VMEM,
        compiler_params=pltpu.CompilerParams(vmem_limit_bytes=LIMIT),
        name="core",
    )(side, weight, kept, received)


def swap(value, axis, size, bit):
    return lax.ppermute(value, axis, [(i, i ^ bit) for i in range(size)])


def across(value, sizes, cell_bit, samp_bit):
    cells, samp = sizes
    pairs = [
        (i * samp + j, (i ^ cell_bit) * samp + (j ^ samp_bit ^ 1))
        for i in range(cells)
        for j in range(samp)
    ]
    return lax.ppermute(value, ("cells", "samp"), pairs)


def bits(size):
    return [1 << b for b in range(size.bit_length() - 1)]


def side_of(blocks, axis, bit, dim):
    mine = (lax.axis_index(axis) // bit) % 2
    return (
        lax.dynamic_index_in_dim(blocks, mine, dim, False),
        lax.dynamic_index_in_dim(blocks, 1 - mine, dim, False),
    )


def halving(blocks, axis, size, bit, dim):
    kept, sent = side_of(blocks, axis, bit, dim)
    return kept, swap(sent, axis, size, bit)


def build(sizes):
    cells, samp = sizes["cells"], sizes["samp"]

    def on_device(snapshots, left_slow, left_fast, right_slow, right_fast):
        height, width = snapshots.shape
        share = width // cells
        chunk = share if share % 128 == 0 else width
        me, cell = lax.axis_index("samp"), lax.axis_index("cells")
        flips = [me >> b for b in range(len(bits(samp)))] + [cell >> b for b in range(len(bits(cells)))]
        half = functools.reduce(lax.bitwise_xor, flips) & 1
        chunks, part, spans = sketches(
            jnp.stack([me, half]), snapshots, left_slow, left_fast, right_slow, right_fast, chunk, samp
        )
        if chunk != share:
            chunks = chunks[0].reshape(-1, cells, share).transpose(1, 0, 2)

        together = lax.optimization_barrier
        sizes, levels = (cells, samp), bits(cells)
        depth = len(levels)
        left = chunks.reshape((2,) * depth + chunks.shape[1:])
        part, left = together((part, left))
        stay, leave = side_of(left, "cells", levels[1], depth - 2)
        leave = sum(halving(leave, "cells", cells, levels[0], depth - 2))
        stay = sum(halving(stay, "cells", cells, levels[0], depth - 2))
        mine = part[0] + swap(part[1], "samp", samp, 1)
        far = spans[3] + swap(spans[2], "samp", samp, 1)
        mine, far = together((mine, far))
        near = spans[0] + swap(spans[1], "samp", samp, 1)
        crossing = swap(far, "samp", samp, 3)
        mine = mine + across(mine, sizes, 0, 2)
        mine, leave = together((mine, leave))
        received = swap(leave, "cells", cells, levels[1])
        mine = paced(mine + across(mine, sizes, levels[1], 0), 10**9)
        mine = mine + across(mine, sizes, levels[0], 0)
        mine, left = together((mine, stay + received))
        kept, received = halving(left, "cells", cells, levels[2], depth - 3)
        mine = paced(mine + across(mine, sizes, levels[2], 0), 10**8)
        for step, bit in enumerate(levels[3:]):
            mine = mine + across(mine, sizes, bit, 0)
            kept, received = halving(kept + received, "cells", cells, bit, depth - 4 - step)
        other = swap(mine, "samp", samp, 1)
        other, range_part = together((other, near + crossing))
        side, weight = factor(half.reshape(1), mine, other, right_slow.shape[0])
        return (range_part.T, finish(side, weight, kept, received))

    return on_device


def solution(mesh):
    placed = (P("cells", "samp"), P(None, "cells"), P(), P(None, "samp"), P())
    return jax.shard_map(
        build(mesh.shape),
        mesh=mesh,
        in_specs=placed,
        out_specs=(P(("cells", "samp"), None), P(None, ("samp", "cells"))),
        check_vma=False,
    )
```

```python
import functools
import math

import jax
import jax.numpy as jnp
from jax import lax
from jax.experimental import pallas as pl
from jax.experimental.pallas import tpu as pltpu
from jax.sharding import PartitionSpec as P

F32 = jnp.float32
BF16 = jnp.bfloat16
HIGHEST = lax.Precision.HIGHEST
SCALE = 2.0**-10
RIDGE = 0.5
VMEM = pl.BlockSpec(memory_space=pltpu.VMEM)
HBM = pl.BlockSpec(memory_space=pltpu.HBM)
LIMIT = 16 * 2**20
AHEAD = 2


def dot(a, b, a_dim, b_dim, precision=None):
    return lax.dot_general(
        a, b, (((a_dim,), (b_dim,)), ((), ())), precision=precision, preferred_element_type=F32
    )


def repeated(factor_t, width, inner, outer):
    count = factor_t.shape[0]
    row = lax.broadcasted_iota(jnp.int32, (count, width), 0)
    column = lax.broadcasted_iota(jnp.int32, (count, width), 1)
    if outer:
        pick = (column >= row * inner) & (column < (row + 1) * inner)
    elif count & (count - 1) == 0:
        pick = (column & (count - 1)) == row
    else:
        pick = lax.rem(column, count) == row
    return dot(factor_t, jnp.where(pick, 1.0, 0.0).astype(BF16), 0, 0)


def expand(slow_t, fast_t):
    inner = fast_t.shape[0]
    width = slow_t.shape[0] * inner
    period = inner * 128 // math.gcd(inner, 128)
    if width % period:
        period = width
    fast = repeated(fast_t, period, 1, False)
    fast = jnp.concatenate([fast] * (width // period), 1)
    return (repeated(slow_t, width, inner, True) * fast).astype(BF16)


def halves(value):
    high = value.astype(BF16)
    return high, (value - high.astype(F32)).astype(BF16)


def sketch_kernel(place, slow, fast, right_slow, right_fast, slab, left, part, spans, *scratch):
    factors, (held, sems, slab_sems) = scratch[:4], scratch[4:]
    count, rank, rows = spans.shape
    starts = [i * rows for i in range(count)]
    copies = [
        pltpu.make_async_copy(source, target, sems.at[i])
        for i, (source, target) in enumerate(zip((slow, fast, right_slow, right_fast), factors))
    ]
    pieces = [
        pltpu.make_async_copy(slab.at[pl.ds(start, rows)], held.at[pl.ds(start, rows)], slab_sems.at[i])
        for i, start in enumerate(starts)
    ]
    for copy in copies:
        copy.start()
    for copy in pieces[:AHEAD]:
        copy.start(priority=1)
    for copy in copies:
        copy.wait()
    omega = expand(factors[2][...], factors[3][...])
    psi = expand(factors[0][...], factors[1][...])
    value = None
    for i, start in enumerate(starts):
        pieces[i].wait()
        if i + AHEAD < count:
            pieces[i + AHEAD].start(priority=1)
        block = held[start : start + rows]
        term = dot(psi[:, start : start + rows], block, 1, 0)
        value = term if value is None else value + term
        if i == count - 1:
            chunk = left.shape[2]
            for c in range(left.shape[0]):
                left[c] = value[:, c * chunk : (c + 1) * chunk]
            high, low = halves(value)
            whole = dot(omega, high, 1, 1) + dot(omega, low, 1, 1)
            half = part.shape[1]
            bit = place[1]
            part[bit] = whole[:half]
            part[bit ^ 1, : rank - half] = whole[half:]
            part[bit ^ 1, rank - half :] = jnp.zeros((2 * half - rank, whole.shape[1]), F32)
        if i % 2:
            pair = dot(omega, held[start - rows : start + rows], 1, 1)
            spans[place[0] ^ (i - 1)] = pair[:, :rows]
            spans[place[0] ^ i] = pair[:, rows:]


def half_of(rank):
    return -(-rank // 16) * 8


def sketches(place, snapshots, left_slow, left_fast, right_slow, right_fast, chunk, count):
    height, width = snapshots.shape
    rank_left, rank_right = left_slow.shape[0], right_slow.shape[0]
    factors = [f.T for f in (left_slow, left_fast, right_slow, right_fast)]
    rows = height // count
    inputs = [pltpu.with_memory_space_constraint(x, pltpu.HBM) for x in factors + [snapshots]]
    return pl.pallas_call(
        sketch_kernel,
        in_specs=[pl.BlockSpec(memory_space=pltpu.SMEM)] + [HBM] * 5,
        out_specs=(VMEM,) * 3,
        out_shape=(
            jax.ShapeDtypeStruct((width // chunk, rank_left, chunk), F32),
            jax.ShapeDtypeStruct((2, half_of(rank_right), rank_left), F32),
            jax.ShapeDtypeStruct((count, rank_right, rows), F32),
        ),
        scratch_shapes=[pltpu.VMEM(f.shape, BF16) for f in factors]
        + [
            pltpu.VMEM(snapshots.shape, BF16),
            pltpu.SemaphoreType.DMA((4,)),
            pltpu.SemaphoreType.DMA((count,)),
        ],
        compiler_params=pltpu.CompilerParams(vmem_limit_bytes=LIMIT),
        cost_estimate=pl.CostEstimate(
            flops=2 * (rank_left + rank_right) * height * width,
            bytes_accessed=2 * height * width,
            transcendentals=0,
        ),
        name="sketches",
    )(place, *inputs)


def row_of(tile, at):
    return jnp.broadcast_to(tile[at : at + 1, :], tile.shape)


def eliminate(gram):
    size = gram.shape[0]
    lane = lax.broadcasted_iota(jnp.int32, (8, size), 1)
    sub = lax.broadcasted_iota(jnp.int32, (8, size), 0)
    tiles = [gram[i : i + 8] for i in range(0, size, 8)]
    scaled = []
    for t in range(len(tiles)):
        k = 8 * t
        live = range(t, len(tiles))
        column = [
            {i: jnp.broadcast_to(tiles[i][:, k + j : k + j + 1], (8, size)) for i in live}
            for j in range(8)
        ]
        inside = (lane >= k) & (lane < k + 8)
        for i in live:
            tiles[i] = jnp.where(inside, 0.0, tiles[i])
        row = [row_of(tiles[t], j) for j in range(8)]
        weight = [None] * 8
        for p in range(0, 8, 2):
            q = p + 1
            a = row_of(column[p][t], p)
            b = row_of(column[q][t], p)
            c = row_of(column[q][t], q)
            det = a * c - b * b
            inverse = pl.reciprocal(det, approx=True)
            a, b, c = c * inverse, -b * inverse, a * inverse
            row[p] = jnp.where(lane == k + p, 1.0, row[p])
            row[q] = jnp.where(lane == k + q, 1.0, row[q])
            weight[p] = a * row[p] + b * row[q]
            weight[q] = b * row[p] + c * row[q]
            for j in range(q + 1, 8):
                f, g = row_of(column[j][t], p), row_of(column[j][t], q)
                u, v = a * f + b * g, b * f + c * g
                column[j] = {
                    i: column[j][i] - (column[p][i] * u + column[q][i] * v) for i in live
                }
                row[j] = row[j] - (
                    row_of(column[p][t], j) * weight[p] + row_of(column[q][t], j) * weight[q]
                )
            for i in live[1:]:
                tiles[i] = tiles[i] - (column[p][i] * weight[p] + column[q][i] * weight[q])
        held, out = row[0], weight[0]
        for j in range(1, 8):
            held = jnp.where(sub == j, row[j], held)
            out = jnp.where(sub == j, weight[j], out)
        tiles[t] = held
        scaled.append(out)
    return jnp.concatenate(tiles, 0), jnp.concatenate(scaled, 0)


def factor_kernel(low_first, mine, other, side, weight):
    first = low_first[0] == 0
    mine, other = mine[...], other[...]
    half = mine.shape[0]
    low, high = jnp.where(first, mine, other), jnp.where(first, other, mine)
    value = jnp.concatenate([low, high[: side.shape[0] - half]], 0) * SCALE
    size = value.shape[1]
    i = lax.broadcasted_iota(jnp.int32, (size, size), 0)
    j = lax.broadcasted_iota(jnp.int32, (size, size), 1)
    gram = dot(value, value, 0, 0, HIGHEST) + jnp.where(i == j, RIDGE * SCALE * SCALE, 0.0)
    lower, scaled = eliminate(gram)
    keep = (j >> 1) <= (i >> 1)
    side[...] = dot3(value, jnp.where(keep, lower, 0.0), 1, 1)
    weight[...] = jnp.where(keep, scaled, 0.0) * SCALE


def factor(low_first, mine, other, rank):
    size = mine.shape[1]
    return pl.pallas_call(
        factor_kernel,
        out_shape=(
            jax.ShapeDtypeStruct((rank, size), F32),
            jax.ShapeDtypeStruct((size, size), F32),
        ),
        in_specs=[pl.BlockSpec(memory_space=pltpu.SMEM)] + [VMEM] * 2,
        out_specs=(VMEM, VMEM),
        compiler_params=pltpu.CompilerParams(vmem_limit_bytes=LIMIT),
        cost_estimate=pl.CostEstimate(flops=10**4, bytes_accessed=1000, transcendentals=0),
        name="factor",
    )(low_first, mine, other)


def pass_on(*refs):
    del refs


def paced(value, pace):
    anywhere = pl.BlockSpec(memory_space=pl.ANY)
    return pl.pallas_call(
        pass_on,
        out_shape=jax.ShapeDtypeStruct(value.shape, value.dtype),
        in_specs=[anywhere],
        out_specs=anywhere,
        input_output_aliases={0: 0},
        compiler_params=pltpu.CompilerParams(vmem_limit_bytes=LIMIT),
        cost_estimate=pl.CostEstimate(flops=pace, bytes_accessed=0, transcendentals=0),
        name="paced",
    )(value)


def dot3(a, b, a_dim, b_dim):
    (a_high, a_low), (b_high, b_low) = halves(a), halves(b)
    small = dot(a_high, b_low, a_dim, b_dim) + dot(a_low, b_high, a_dim, b_dim)
    return dot(a_high, b_high, a_dim, b_dim) + small


def core_kernel(side, weight, kept, received, core):
    left = kept[...] + received[...]
    core[...] = dot3(side[...], dot3(weight[...], left, 1, 0), 1, 0)


def finish(side, weight, kept, received):
    return pl.pallas_call(
        core_kernel,
        out_shape=jax.ShapeDtypeStruct((side.shape[0], kept.shape[1]), F32),
        in_specs=[VMEM] * 4,
        out_specs=VMEM,
        compiler_params=pltpu.CompilerParams(vmem_limit_bytes=LIMIT),
        name="core",
    )(side, weight, kept, received)


def swap(value, axis, size, bit):
    return lax.ppermute(value, axis, [(i, i ^ bit) for i in range(size)])


def across(value, sizes, cell_bit, samp_bit):
    cells, samp = sizes
    pairs = [
        (i * samp + j, (i ^ cell_bit) * samp + (j ^ samp_bit ^ 1))
        for i in range(cells)
        for j in range(samp)
    ]
    return lax.ppermute(value, ("cells", "samp"), pairs)


def bits(size):
    return [1 << b for b in range(size.bit_length() - 1)]


def side_of(blocks, axis, bit, dim):
    mine = (lax.axis_index(axis) // bit) % 2
    return (
        lax.dynamic_index_in_dim(blocks, mine, dim, False),
        lax.dynamic_index_in_dim(blocks, 1 - mine, dim, False),
    )


def halving(blocks, axis, size, bit, dim):
    kept, sent = side_of(blocks, axis, bit, dim)
    return kept, swap(sent, axis, size, bit)


def build(sizes):
    cells, samp = sizes["cells"], sizes["samp"]

    def on_device(snapshots, left_slow, left_fast, right_slow, right_fast):
        height, width = snapshots.shape
        share = width // cells
        chunk = share if share % 128 == 0 else width
        me, cell = lax.axis_index("samp"), lax.axis_index("cells")
        flips = [me >> b for b in range(len(bits(samp)))] + [cell >> b for b in range(len(bits(cells)))]
        half = functools.reduce(lax.bitwise_xor, flips) & 1
        chunks, part, spans = sketches(
            jnp.stack([me, half]), snapshots, left_slow, left_fast, right_slow, right_fast, chunk, samp
        )
        if chunk != share:
            chunks = chunks[0].reshape(-1, cells, share).transpose(1, 0, 2)

        together = lax.optimization_barrier
        sizes, levels = (cells, samp), bits(cells)
        depth = len(levels)
        left = chunks.reshape((2,) * depth + chunks.shape[1:])
        part, left = together((part, left))
        stay, leave = side_of(left, "cells", levels[1], depth - 2)
        leave = sum(halving(leave, "cells", cells, levels[0], depth - 2))
        stay = sum(halving(stay, "cells", cells, levels[0], depth - 2))
        mine = part[0] + swap(part[1], "samp", samp, 1)
        far = spans[3] + swap(spans[2], "samp", samp, 1)
        mine, far = together((mine, far))
        near = spans[0] + swap(spans[1], "samp", samp, 1)
        crossing = swap(far, "samp", samp, 3)
        mine = mine + across(mine, sizes, 0, 2)
        mine, leave = together((mine, leave))
        received = swap(leave, "cells", cells, levels[1])
        mine = paced(mine + across(mine, sizes, levels[1], 0), 10**9)
        mine = mine + across(mine, sizes, levels[0], 0)
        mine, left = together((mine, stay + received))
        kept, received = halving(left, "cells", cells, levels[2], depth - 3)
        mine = paced(mine + across(mine, sizes, levels[2], 0), 10**8)
        for step, bit in enumerate(levels[3:]):
            mine = mine + across(mine, sizes, bit, 0)
            kept, received = halving(kept + received, "cells", cells, bit, depth - 4 - step)
        other = swap(mine, "samp", samp, 1)
        other, range_part = together((other, near + crossing))
        side, weight = factor(half.reshape(1), mine, other, right_slow.shape[0])
        return (range_part.T, finish(side, weight, kept, received))

    return on_device


def solution(mesh):
    placed = (P("cells", "samp"), P(None, "cells"), P(), P(None, "samp"), P())
    return jax.shard_map(
        build(mesh.shape),
        mesh=mesh,
        in_specs=placed,
        out_specs=(P(("cells", "samp"), None), P(None, ("samp", "cells"))),
        check_vma=False,
    )
```

```python
import functools
import math

import jax
import jax.numpy as jnp
from jax import lax
from jax.experimental import pallas as pl
from jax.experimental.pallas import tpu as pltpu
from jax.sharding import PartitionSpec as P

F32 = jnp.float32
BF16 = jnp.bfloat16
HIGHEST = lax.Precision.HIGHEST
SCALE = 2.0**-10
RIDGE = 0.5
VMEM = pl.BlockSpec(memory_space=pltpu.VMEM)
HBM = pl.BlockSpec(memory_space=pltpu.HBM)
LIMIT = 16 * 2**20
AHEAD = 2


def dot(a, b, a_dim, b_dim, precision=None):
    return lax.dot_general(
        a, b, (((a_dim,), (b_dim,)), ((), ())), precision=precision, preferred_element_type=F32
    )


def repeated(factor_t, width, inner, outer):
    count = factor_t.shape[0]
    row = lax.broadcasted_iota(jnp.int32, (count, width), 0)
    column = lax.broadcasted_iota(jnp.int32, (count, width), 1)
    if outer:
        pick = (column >= row * inner) & (column < (row + 1) * inner)
    elif count & (count - 1) == 0:
        pick = (column & (count - 1)) == row
    else:
        pick = lax.rem(column, count) == row
    return dot(factor_t, jnp.where(pick, 1.0, 0.0).astype(BF16), 0, 0)


def expand(slow_t, fast_t):
    inner = fast_t.shape[0]
    width = slow_t.shape[0] * inner
    period = inner * 128 // math.gcd(inner, 128)
    if width % period:
        period = width
    fast = repeated(fast_t, period, 1, False)
    fast = jnp.concatenate([fast] * (width // period), 1)
    return (repeated(slow_t, width, inner, True) * fast).astype(BF16)


def halves(value):
    high = value.astype(BF16)
    return high, (value - high.astype(F32)).astype(BF16)


def sketch_kernel(place, slow, fast, right_slow, right_fast, slab, left, part, spans, *scratch):
    factors, (held, sems, slab_sems) = scratch[:4], scratch[4:]
    count, rank, rows = spans.shape
    starts = [i * rows for i in range(count)]
    copies = [
        pltpu.make_async_copy(source, target, sems.at[i])
        for i, (source, target) in enumerate(zip((slow, fast, right_slow, right_fast), factors))
    ]
    pieces = [
        pltpu.make_async_copy(slab.at[pl.ds(start, rows)], held.at[pl.ds(start, rows)], slab_sems.at[i])
        for i, start in enumerate(starts)
    ]
    for copy in copies:
        copy.start()
    for copy in pieces[:AHEAD]:
        copy.start(priority=1)
    for copy in copies:
        copy.wait()
    psi = expand(factors[0][...], factors[1][...])
    value = None
    for i, start in enumerate(starts):
        if i == 1:
            omega = expand(factors[2][...], factors[3][...])
        pieces[i].wait()
        if i + AHEAD < count:
            pieces[i + AHEAD].start(priority=1)
        block = held[start : start + rows]
        term = dot(psi[:, start : start + rows], block, 1, 0)
        value = term if value is None else value + term
        if i == count - 1:
            chunk = left.shape[2]
            for c in range(left.shape[0]):
                left[c] = value[:, c * chunk : (c + 1) * chunk]
            high, low = halves(value)
            whole = dot(omega, high, 1, 1) + dot(omega, low, 1, 1)
            half = part.shape[1]
            bit = place[1]
            part[bit] = whole[:half]
            part[bit ^ 1, : rank - half] = whole[half:]
            part[bit ^ 1, rank - half :] = jnp.zeros((2 * half - rank, whole.shape[1]), F32)
        if i % 2:
            pair = dot(omega, held[start - rows : start + rows], 1, 1)
            spans[place[0] ^ (i - 1)] = pair[:, :rows]
            spans[place[0] ^ i] = pair[:, rows:]


def half_of(rank):
    return -(-rank // 16) * 8


def sketches(place, snapshots, left_slow, left_fast, right_slow, right_fast, chunk, count):
    height, width = snapshots.shape
    rank_left, rank_right = left_slow.shape[0], right_slow.shape[0]
    factors = [f.T for f in (left_slow, left_fast, right_slow, right_fast)]
    rows = height // count
    inputs = [pltpu.with_memory_space_constraint(x, pltpu.HBM) for x in factors + [snapshots]]
    return pl.pallas_call(
        sketch_kernel,
        in_specs=[pl.BlockSpec(memory_space=pltpu.SMEM)] + [HBM] * 5,
        out_specs=(VMEM,) * 3,
        out_shape=(
            jax.ShapeDtypeStruct((width // chunk, rank_left, chunk), F32),
            jax.ShapeDtypeStruct((2, half_of(rank_right), rank_left), F32),
            jax.ShapeDtypeStruct((count, rank_right, rows), F32),
        ),
        scratch_shapes=[pltpu.VMEM(f.shape, BF16) for f in factors]
        + [
            pltpu.VMEM(snapshots.shape, BF16),
            pltpu.SemaphoreType.DMA((4,)),
            pltpu.SemaphoreType.DMA((count,)),
        ],
        compiler_params=pltpu.CompilerParams(vmem_limit_bytes=LIMIT),
        cost_estimate=pl.CostEstimate(
            flops=2 * (rank_left + rank_right) * height * width,
            bytes_accessed=2 * height * width,
            transcendentals=0,
        ),
        name="sketches",
    )(place, *inputs)


def row_of(tile, at):
    return jnp.broadcast_to(tile[at : at + 1, :], tile.shape)


def eliminate(gram):
    size = gram.shape[0]
    lane = lax.broadcasted_iota(jnp.int32, (8, size), 1)
    sub = lax.broadcasted_iota(jnp.int32, (8, size), 0)
    tiles = [gram[i : i + 8] for i in range(0, size, 8)]
    scaled = []
    for t in range(len(tiles)):
        k = 8 * t
        live = range(t, len(tiles))
        column = [
            {i: jnp.broadcast_to(tiles[i][:, k + j : k + j + 1], (8, size)) for i in live}
            for j in range(8)
        ]
        inside = (lane >= k) & (lane < k + 8)
        for i in live:
            tiles[i] = jnp.where(inside, 0.0, tiles[i])
        row = [row_of(tiles[t], j) for j in range(8)]
        weight = [None] * 8
        for p in range(0, 8, 2):
            q = p + 1
            a = row_of(column[p][t], p)
            b = row_of(column[q][t], p)
            c = row_of(column[q][t], q)
            det = a * c - b * b
            inverse = pl.reciprocal(det, approx=True)
            a, b, c = c * inverse, -b * inverse, a * inverse
            row[p] = jnp.where(lane == k + p, 1.0, row[p])
            row[q] = jnp.where(lane == k + q, 1.0, row[q])
            weight[p] = a * row[p] + b * row[q]
            weight[q] = b * row[p] + c * row[q]
            for j in range(q + 1, 8):
                f, g = row_of(column[j][t], p), row_of(column[j][t], q)
                u, v = a * f + b * g, b * f + c * g
                column[j] = {
                    i: column[j][i] - (column[p][i] * u + column[q][i] * v) for i in live
                }
                row[j] = row[j] - (
                    row_of(column[p][t], j) * weight[p] + row_of(column[q][t], j) * weight[q]
                )
            for i in live[1:]:
                tiles[i] = tiles[i] - (column[p][i] * weight[p] + column[q][i] * weight[q])
        held, out = row[0], weight[0]
        for j in range(1, 8):
            held = jnp.where(sub == j, row[j], held)
            out = jnp.where(sub == j, weight[j], out)
        tiles[t] = held
        scaled.append(out)
    return jnp.concatenate(tiles, 0), jnp.concatenate(scaled, 0)


def factor_kernel(low_first, mine, other, side, weight):
    first = low_first[0] == 0
    mine, other = mine[...], other[...]
    half = mine.shape[0]
    low, high = jnp.where(first, mine, other), jnp.where(first, other, mine)
    value = jnp.concatenate([low, high[: side.shape[0] - half]], 0) * SCALE
    size = value.shape[1]
    i = lax.broadcasted_iota(jnp.int32, (size, size), 0)
    j = lax.broadcasted_iota(jnp.int32, (size, size), 1)
    gram = dot(value, value, 0, 0, HIGHEST) + jnp.where(i == j, RIDGE * SCALE * SCALE, 0.0)
    lower, scaled = eliminate(gram)
    keep = (j >> 1) <= (i >> 1)
    side[...] = dot3(value, jnp.where(keep, lower, 0.0), 1, 1)
    weight[...] = jnp.where(keep, scaled, 0.0) * SCALE


def factor(low_first, mine, other, rank):
    size = mine.shape[1]
    return pl.pallas_call(
        factor_kernel,
        out_shape=(
            jax.ShapeDtypeStruct((rank, size), F32),
            jax.ShapeDtypeStruct((size, size), F32),
        ),
        in_specs=[pl.BlockSpec(memory_space=pltpu.SMEM)] + [VMEM] * 2,
        out_specs=(VMEM, VMEM),
        compiler_params=pltpu.CompilerParams(vmem_limit_bytes=LIMIT),
        cost_estimate=pl.CostEstimate(flops=10**4, bytes_accessed=1000, transcendentals=0),
        name="factor",
    )(low_first, mine, other)


def pass_on(*refs):
    del refs


def paced(value, pace):
    anywhere = pl.BlockSpec(memory_space=pl.ANY)
    return pl.pallas_call(
        pass_on,
        out_shape=jax.ShapeDtypeStruct(value.shape, value.dtype),
        in_specs=[anywhere],
        out_specs=anywhere,
        input_output_aliases={0: 0},
        compiler_params=pltpu.CompilerParams(vmem_limit_bytes=LIMIT),
        cost_estimate=pl.CostEstimate(flops=pace, bytes_accessed=0, transcendentals=0),
        name="paced",
    )(value)


def dot3(a, b, a_dim, b_dim):
    (a_high, a_low), (b_high, b_low) = halves(a), halves(b)
    small = dot(a_high, b_low, a_dim, b_dim) + dot(a_low, b_high, a_dim, b_dim)
    return dot(a_high, b_high, a_dim, b_dim) + small


def core_kernel(side, weight, kept, received, core):
    left = kept[...] + received[...]
    core[...] = dot3(side[...], dot3(weight[...], left, 1, 0), 1, 0)


def finish(side, weight, kept, received):
    return pl.pallas_call(
        core_kernel,
        out_shape=jax.ShapeDtypeStruct((side.shape[0], kept.shape[1]), F32),
        in_specs=[VMEM] * 4,
        out_specs=VMEM,
        compiler_params=pltpu.CompilerParams(vmem_limit_bytes=LIMIT),
        name="core",
    )(side, weight, kept, received)


def swap(value, axis, size, bit):
    return lax.ppermute(value, axis, [(i, i ^ bit) for i in range(size)])


def across(value, sizes, cell_bit, samp_bit):
    cells, samp = sizes
    pairs = [
        (i * samp + j, (i ^ cell_bit) * samp + (j ^ samp_bit ^ 1))
        for i in range(cells)
        for j in range(samp)
    ]
    return lax.ppermute(value, ("cells", "samp"), pairs)


def bits(size):
    return [1 << b for b in range(size.bit_length() - 1)]


def side_of(blocks, axis, bit, dim):
    mine = (lax.axis_index(axis) // bit) % 2
    return (
        lax.dynamic_index_in_dim(blocks, mine, dim, False),
        lax.dynamic_index_in_dim(blocks, 1 - mine, dim, False),
    )


def halving(blocks, axis, size, bit, dim):
    kept, sent = side_of(blocks, axis, bit, dim)
    return kept, swap(sent, axis, size, bit)


def build(sizes):
    cells, samp = sizes["cells"], sizes["samp"]

    def on_device(snapshots, left_slow, left_fast, right_slow, right_fast):
        height, width = snapshots.shape
        share = width // cells
        chunk = share if share % 128 == 0 else width
        me, cell = lax.axis_index("samp"), lax.axis_index("cells")
        flips = [me >> b for b in range(len(bits(samp)))] + [cell >> b for b in range(len(bits(cells)))]
        half = functools.reduce(lax.bitwise_xor, flips) & 1
        chunks, part, spans = sketches(
            jnp.stack([me, half]), snapshots, left_slow, left_fast, right_slow, right_fast, chunk, samp
        )
        if chunk != share:
            chunks = chunks[0].reshape(-1, cells, share).transpose(1, 0, 2)

        together = lax.optimization_barrier
        sizes, levels = (cells, samp), bits(cells)
        depth = len(levels)
        left = chunks.reshape((2,) * depth + chunks.shape[1:])
        part, left = together((part, left))
        stay, leave = side_of(left, "cells", levels[1], depth - 2)
        leave = sum(halving(leave, "cells", cells, levels[0], depth - 2))
        stay = sum(halving(stay, "cells", cells, levels[0], depth - 2))
        mine = part[0] + swap(part[1], "samp", samp, 1)
        far = spans[3] + swap(spans[2], "samp", samp, 1)
        mine, far = together((mine, far))
        near = spans[0] + swap(spans[1], "samp", samp, 1)
        crossing = swap(far, "samp", samp, 3)
        mine = mine + across(mine, sizes, 0, 2)
        mine, leave = together((mine, leave))
        received = swap(leave, "cells", cells, levels[1])
        mine = paced(mine + across(mine, sizes, levels[1], 0), 10**9)
        mine = mine + across(mine, sizes, levels[0], 0)
        mine, left = together((mine, stay + received))
        kept, received = halving(left, "cells", cells, levels[2], depth - 3)
        mine = paced(mine + across(mine, sizes, levels[2], 0), 10**8)
        for step, bit in enumerate(levels[3:]):
            mine = mine + across(mine, sizes, bit, 0)
            kept, received = halving(kept + received, "cells", cells, bit, depth - 4 - step)
        other = swap(mine, "samp", samp, 1)
        other, range_part = together((other, near + crossing))
        side, weight = factor(half.reshape(1), mine, other, right_slow.shape[0])
        return (range_part.T, finish(side, weight, kept, received))

    return on_device


def solution(mesh):
    placed = (P("cells", "samp"), P(None, "cells"), P(), P(None, "samp"), P())
    return jax.shard_map(
        build(mesh.shape),
        mesh=mesh,
        in_specs=placed,
        out_specs=(P(("cells", "samp"), None), P(None, ("samp", "cells"))),
        check_vma=False,
    )
```
